512 devices in a mesh: row: 32 (over z_lo, x, core), col: 16 (over z_hi, y).
Axes of the slice: x: 4, y: 8, z: 8 (z_hi: 2, z_lo: 4; z = z_hi * 4 + z_lo), core: 2. Of those that a mesh axis runs over, the one named last changes fastest.
Arguments:
- ingest: bfloat16 [8192, 32768], P(('row', 'col')), may hold values from -128 to 127, as said below
- row_order: int32 [32, 256], P('row'), may hold values from 0 to 255, each once within a row
- matrix_seeds: int32 [2], replicated, may hold values from 0 to 46336
Outputs:
- second_hint: float32 [4, 2, 1024, 1024], P(None, None, 'col')
The draws below stay inside these ranges and needn't reach their ends.
Inputs may be any that keep to these rules, and one draw needn't show every extreme that they name: `ingest`: integers. `row_order`: each row is a permutation of 0 to 255.
All inputs are finite; a program needn't handle non-finite values.
Results may differ from the reference program's by a relative error of at most 0.0003.
Values may be sent and summed in bfloat16 or wider, within the bound.
A program may use at most 64 MiB of HBM per device.

```python
import jax
import jax.numpy as jnp
from jax import lax

N = 1024
RD = 256
ROWS = 8192
COLS = 32768
RBLK = 32


def draw_ingest(key, part):
    values = jax.random.randint(key, (ROWS, COLS), -128, 128, dtype=jnp.int32)
    return values.astype(jnp.float32).astype(jnp.bfloat16)


def setup_inputs(seed: int = 0) -> dict:
    seeds = jax.random.split(jax.random.key(seed), 4)
    ingest = draw_ingest(jax.random.fold_in(seeds[3], 71), 0)
    row_order = jax.vmap(lambda own: jax.random.permutation(own, RD))(jax.random.split(seeds[1], RBLK)).reshape((RBLK, RD)).astype(jnp.int32)
    matrix_seeds = jax.random.randint(seeds[2], (2,), 0, 46337).astype(jnp.int32)
    return dict(ingest=ingest, row_order=row_order, matrix_seeds=matrix_seeds)


prime_base = 46337
half_scale = 65536.0


def mixed_value(first_index, second_index, seed_value):
    mixed = (first_index % prime_base * 40503 % prime_base + seed_value) % prime_base
    mixed = (mixed * mixed % prime_base + second_index % prime_base * 29989 % prime_base) % prime_base
    return (mixed * mixed % prime_base + 12345) % prime_base


def seeded_quad(first_index, second_index, seed_value):
    first_mix = mixed_value(first_index, second_index, seed_value)
    second_mix = mixed_value(first_index, second_index, seed_value + 7919)
    pieces = [first_mix % 256, first_mix // 256, second_mix % 256, second_mix // 256]
    return [(piece - 128).astype(jnp.float32).astype(jnp.bfloat16) for piece in pieces]


def combine_limbs(products):
    total = products[0].astype(jnp.int32)
    for place in range(1, 4):
        total = total + products[place].astype(jnp.int32) * jnp.int32(256 ** place)
    return total


def signed_bytes(value):
    return [((lax.shift_right_logical(value, jnp.int32(8 * place)) & 255) - 128).astype(jnp.float32).astype(jnp.bfloat16) for place in range(4)]


def halves(value):
    low_half = (value & 65535).astype(jnp.float32)
    high_half = lax.shift_right_logical(value, jnp.int32(16)).astype(jnp.float32)
    return low_half, high_half


def reference(ingest, row_order, matrix_seeds):
    row_total, col_total = ingest.shape
    col_index = lax.broadcasted_iota(jnp.int32, (col_total, N), 0)
    n_index = lax.broadcasted_iota(jnp.int32, (col_total, N), 1)
    quad_one = jnp.stack(seeded_quad(col_index, n_index, matrix_seeds[0]))
    col_width = min(512, col_total)

    def block_hint(block_number):
        block_rows = lax.dynamic_slice_in_dim(ingest, block_number * RD, RD, 0)
        block_rows = jnp.take(block_rows, row_order[block_number], axis=0)

        def advance(turn_index, running):
            start_col = (turn_index * col_width).astype(jnp.int32)
            piece = lax.dynamic_slice_in_dim(block_rows, start_col, col_width, 1)
            quad_slice = lax.dynamic_slice_in_dim(quad_one, start_col, col_width, 1)
            products = [jnp.dot(piece, quad_slice[place], preferred_element_type=jnp.float32) for place in range(4)]
            return running + combine_limbs(products)

        return lax.fori_loop(0, col_total // col_width, advance, jnp.zeros((RD, N), jnp.int32))

    hint = lax.map(block_hint, jnp.arange(row_total // RD, dtype=jnp.int32)).reshape(row_total, N)
    digits = jnp.stack(signed_bytes(hint))
    row_index = lax.broadcasted_iota(jnp.int32, (row_total, N), 0)
    m_index = lax.broadcasted_iota(jnp.int32, (row_total, N), 1)
    quad_two = jnp.stack(seeded_quad(row_index, m_index, matrix_seeds[1]))
    row_width = min(512, row_total)

    def accumulate(turn_index, running):
        start_row = (turn_index * row_width).astype(jnp.int32)
        quad_slice = lax.dynamic_slice_in_dim(quad_two, start_row, row_width, 1)
        digit_block = lax.dynamic_slice_in_dim(digits, start_row, row_width, 1)
        terms = []
        for digit_place in range(4):
            products = [jnp.dot(quad_slice[place].T, digit_block[digit_place], preferred_element_type=jnp.float32) for place in range(4)]
            terms.append(combine_limbs(products))
        return running + jnp.stack(terms, axis=1)

    total = lax.fori_loop(0, row_total // row_width, accumulate, jnp.zeros((N, 4, N), jnp.int32))
    total = jnp.transpose(total, (1, 2, 0))
    low_half, high_half = halves(total)
    return jnp.stack([low_half, high_half], axis=1) / half_scale
```

```python
import functools

import jax
import jax.numpy as jnp
from jax import lax
from jax.experimental import pallas as pl
from jax.experimental.pallas import tpu as pltpu
from jax.sharding import PartitionSpec as P

PRIME = 46337
HALF = 23168
INV = 1.0 / PRIME
MAGIC_ONE = 1.5 * 2.0**23
MAGIC_BYTE = 1.5 * 2.0**31
BIAS = (HALF * 65537 - 0x80808080) % 2**32
BIAS = BIAS - 2**32 if BIAS >= 2**31 else BIAS
NEAR = ((0, 0, 0), (0, 1, 0), (1, 0, 0), (0, 0, 1), (0, 1, 1), (0, 0, -1), (-1, 0, 0), (0, -1, 0))
ORDER = (4, 1, 2, 3, 5, 6, 7, 0)
MESH = pl.DeviceIdType.MESH
F32, BF16, I32 = jnp.float32, jnp.bfloat16, jnp.int32
NT = (((1,), (1,)), ((), ()))
NN = (((1,), (0,)), ((), ()))


def modp(v):
    q = (v.astype(F32) * INV).astype(I32)
    r = v - q * PRIME
    r = jnp.where(r < 0, r + PRIME, r)
    return jnp.where(r >= PRIME, r - PRIME, r)


def centred(v):
    return jnp.where(v > HALF, v - PRIME, v)


def two_digits(v):
    hi = ((v + 128 + 65536) // 256 - 256) * 256
    return hi, v - hi


def pick_rows(rows, shape):
    at = lax.broadcasted_iota(I32, shape, 0)
    out = jnp.zeros(shape, I32)
    for k, row in enumerate(rows):
        out = jnp.where(at == k, row, out)
    return out.astype(F32)


def index_digits(index, seed):
    x = modp(modp(index * 40503) + seed)
    x = modp(x * x)
    hi, lo = two_digits(centred(modp(x * x)))
    nib = [lax.shift_right_logical(x, jnp.int32(4 * k)) & 15 for k in range(4)]
    one = jnp.ones_like(x)
    return pick_rows(nib + nib + [hi, lo, one, one], (16, index.shape[1]))


def column_digits(index):
    b = modp(index * 29989)
    his, los = [], []
    w = modp(b + b)
    for k in range(4):
        hi, lo = two_digits(centred(w))
        his.append(hi)
        los.append(lo)
        w = modp(w * 16)
    hi, lo = two_digits(centred(modp(modp(b * b) + (12345 - HALF + PRIME))))
    one = jnp.ones_like(b)
    return pick_rows(his + los + [one, one, hi, lo], (16, index.shape[1]))


def residue_digits(v):
    q = (v * INV + MAGIC_ONE) - MAGIC_ONE
    r = v - q * PRIME
    hi = (r + MAGIC_BYTE) - MAGIC_BYTE
    return (r - hi).astype(BF16), hi.astype(BF16)


def joined(parts):
    t = parts[0].astype(I32)
    t = t + lax.shift_left((parts[1] * (1.0 / 256)).astype(I32), jnp.int32(8))
    t = t + lax.shift_left(parts[2].astype(I32), jnp.int32(16))
    return t + lax.shift_left((parts[3] * (1.0 / 256)).astype(I32), jnp.int32(24))


def kernel(
    seeds, ingest, order, out,
    rec, orders, bdig, xdig, gen_a, gen_b, part, sib, red, hint_send, hint_in, a2, tot, xbuf, xsum, zbuf, full,
    s_in, r_in, s_ord, r_ord, s_sib, r_sib, s_red, r_red, s_hint, r_hint, s_x, r_x, s_z, r_z, s_gz, r_gz, s_gx, r_gx,
    s_gs, r_gs, s_out,
):
    row, col = lax.axis_index("row"), lax.axis_index("col")
    core, x, zl = row % 2, (row // 2) % 4, row // 8
    y, zh = col % 8, col // 8
    z = zh * 4 + zl

    def dev(dx, dy, dz, other):
        xx, yy, zz = (x + dx + 4) % 4, (y + dy + 8) % 8, (z + dz + 8) % 8
        cc = (core + other) % 2
        return {"row": ((zz % 4) * 4 + xx) * 2 + cc, "col": (zz // 4) * 8 + yy}

    def dev_line(dz):
        return {"row": (((zl + dz) % 4) * 4 + x) * 2 + core, "col": col}

    def rcopy(src, dst, ssem, rsem, device):
        return pltpu.make_async_remote_copy(
            src_ref=src, dst_ref=dst, send_sem=ssem, recv_sem=rsem, device_id=device, device_id_type=MESH
        )

    sibling = dev(0, 0, 0, 1)

    barrier = pltpu.get_barrier_semaphore()

    def greet(device):
        pl.semaphore_signal(barrier, inc=1, device_id=device, device_id_type=MESH)

    count = 0
    for off in ((1, 0, 0), (-1, 0, 0), (0, 0, 1), (0, 0, -1), (0, 1, 1), (0, -1, -1)):
        for other in range(2):
            greet(dev(*off, other))
            count += 1
    greet(dev(2, 0, 0, 0))
    count += 1
    for dz in range(1, 4):
        greet(dev_line(dz))
        count += 1

    def greet_col(k, carry):
        greet({"row": row - core + (core + k) % 2, "col": (col + k // 2) % 16})
        return carry

    lax.fori_loop(1, 32, greet_col, 0)
    pl.semaphore_wait(barrier, count + 31)

    colour = (2 * x + y + 3 * z) % 8

    def ingest_src(near, other):
        return ingest.at[:, pl.ds(((colour + near) % 8) * 4096 + ((core + other) % 2) * 2048, 2048)]

    def ingest_copy(near, other):
        slot = near * 2 + core
        return rcopy(
            ingest_src(near, other), rec.at[pl.ds(slot * 16, 16), :],
            s_in.at[near * 2 + other], r_in.at[slot], dev(*NEAR[near], other),
        )

    for near in ORDER:
        for other in range(2):
            if near or other:
                ingest_copy(near, other).start()
    own_in = pltpu.make_async_copy(ingest_src(0, 0), rec.at[pl.ds(core * 16, 16), :], r_in.at[core])
    own_in.start()
    orders[core] = jnp.broadcast_to(order[...], (8, 256))
    order_copy = rcopy(orders.at[core], orders.at[core], s_ord, r_ord, sibling)
    order_copy.start()

    bdig[...] = jnp.transpose(column_digits(lax.broadcasted_iota(I32, (1, 1024), 1))).astype(BF16)
    col_start = colour * 4096 + core * 2048
    index = lax.broadcasted_iota(I32, (1, 2048), 1) + col_start
    for w in range(2):
        xdig[w] = index_digits(index, seeds[0] + 7919 * w).astype(BF16)

    rcopy(orders.at[1 - core], orders.at[1 - core], s_ord, r_ord, sibling).wait_recv()

    half = pl.ds(pl.multiple_of(core * 512, 512), 512)
    for blk in range(2):
        rows_i = (row - core + blk) * 256 + lax.broadcasted_iota(I32, (1, 256), 1)
        onehot = (lax.broadcasted_iota(I32, (256, 256), 0) == orders[blk, 0:1, :]).astype(F32).astype(BF16)
        for w in range(2):
            dig = index_digits(rows_i, seeds[1] + 7919 * w).astype(BF16)
            perm = lax.dot_general(onehot, dig, NT, preferred_element_type=F32).astype(BF16)
            v = lax.dot_general(perm, bdig[half, :], NT, preferred_element_type=F32)
            lo, hi = residue_digits(v)
            a2[2 * w, blk * 256 : (blk + 1) * 256, :] = lo
            a2[2 * w + 1, blk * 256 : (blk + 1) * 256, :] = hi

    def generate(buf, t, kh):
        n_at = pl.multiple_of((((1 - core) * 2 + t) % 4) * 256, 256)
        left = bdig[pl.ds(n_at, 256), :]
        for w in range(2):
            v = lax.dot_general(left, xdig[w, :, kh * 1024 : (kh + 1) * 1024], NN, preferred_element_type=F32)
            lo, hi = residue_digits(v)
            buf[(2 * w) * 256 : (2 * w + 1) * 256, :] = lo
            buf[(2 * w + 1) * 256 : (2 * w + 2) * 256, :] = hi

    def multiply(buf, kh):
        r = lax.dot_general(buf[...], rec[:, kh * 1024 : (kh + 1) * 1024], NT, preferred_element_type=F32)
        return joined([r[k * 256 : (k + 1) * 256, :] for k in range(4)])

    generate(gen_a, 0, 0)
    for slot in range(16):
        rcopy(
            rec.at[pl.ds(slot * 16, 16), :], rec.at[pl.ds(slot * 16, 16), :], s_in.at[0], r_in.at[slot], sibling
        ).wait_recv()
    sums = lax.dot_general(jnp.ones((16, 2048), BF16), rec[...], NT, preferred_element_type=F32)
    bias = sums[0:1, :].astype(I32) * jnp.int32(BIAS)

    sib_copy = rcopy(part.at[1 - core], sib, s_sib, r_sib, sibling)

    def tile(t, carry):
        generate(gen_b, t, 1)
        acc = multiply(gen_a, 0)
        generate(gen_a, t + 1, 0)
        acc = acc + multiply(gen_b, 1) + bias
        part[(1 - core + t // 2) % 2, :, pl.ds(pl.multiple_of((t % 2) * 256, 256), 256)] = jnp.transpose(acc)

        @pl.when(t == 1)
        def _():
            sib_copy.start()

        return carry

    lax.fori_loop(0, 4, tile, 0)
    sib_copy.wait_recv()
    mine = part.at[core]
    mine[...] = mine[...] + sib[...]

    def red_copy(near):
        dx, dy, dz = NEAR[near]
        return rcopy(
            mine.at[pl.ds(near * 32, 32), :], red.at[near], s_red.at[near], r_red.at[near], dev(-dx, -dy, -dz, 0)
        )

    for near in ORDER[:-1]:
        red_copy(near).start()
    hint = mine[0:32, :]
    for near in range(1, 8):
        red_copy(near).wait_recv()
        hint = hint + red[near]

    low_lane = lax.broadcasted_iota(I32, (16, 128), 1) < 64
    for t in range(4):
        top, low = hint[0:16, t * 128 : (t + 1) * 128], hint[16:32, t * 128 : (t + 1) * 128]
        hint_send[2 * t] = jnp.where(low_lane, top, pltpu.roll(low, 64, 1))
        hint_send[2 * t + 1] = jnp.where(low_lane, pltpu.roll(top, 64, 1), low)
    landing = hint_in.at[pl.ds(col * 16, 16), :]
    local = zh == core

    def hint_copy(dy, other):
        yy = (y + dy) % 8
        return rcopy(
            hint_send.at[yy], landing, s_hint.at[dy * 2 + other], r_hint.at[col],
            {"row": row - core + (core + other) % 2, "col": core * 8 + yy},
        )

    own_hint = pltpu.make_async_copy(hint_send.at[y], landing, r_hint.at[col])
    for dy in (4, 3, 5, 2, 6, 1, 7, 0):
        for other in range(2):
            if dy or other:
                hint_copy(dy, other).start()
            else:
                @pl.when(local)
                def _():
                    own_hint.start()

                @pl.when(jnp.logical_not(local))
                def _():
                    hint_copy(0, 0).start()

    for c in range(16):
        spot = hint_in.at[pl.ds(c * 16, 16), :]
        rcopy(spot, spot, s_hint.at[0], r_hint.at[c], sibling).wait_recv()

    turned = jnp.transpose(hint_in[...])
    wide = jnp.concatenate([turned[0:64, :], turned[64:128, :]], axis=1)
    left = jnp.concatenate(
        [
            ((lax.shift_right_logical(wide, jnp.int32(8 * d)) & 255) - 128).astype(F32).astype(BF16)
            for d in range(4)
        ],
        axis=0,
    )
    lsum = lax.dot_general(left, jnp.ones((512, 128), BF16), NN, preferred_element_type=F32)
    lbias = lsum[:, 0:1].astype(I32) * jnp.int32(BIAS)
    tot[...] = joined([lax.dot_general(left, a2[k], NN, preferred_element_type=F32) for k in range(4)]) + lbias

    def x_copy(dx):
        xx = (x + dx) % 4
        return rcopy(tot.at[pl.ds(xx * 64, 64), :], xbuf.at[dx - 1], s_x.at[dx - 1], r_x.at[dx - 1], dev(dx, 0, 0, 0))

    def z_copy(dz):
        zz = (zl + dz) % 4
        return rcopy(xsum.at[pl.ds(zz * 16, 16), :], zbuf.at[dz - 1], s_z.at[dz - 1], r_z.at[dz - 1], dev_line(dz))

    for dx in (2, 1, 3):
        x_copy(dx).start()
    acc = tot[pl.ds(pl.multiple_of(x * 64, 64), 64), :]
    for dx in (1, 3, 2):
        x_copy(dx).wait_recv()
        acc = acc + xbuf[dx - 1]
    xsum[...] = acc
    for dz in (1, 3, 2):
        z_copy(dz).start()
    acc = xsum[pl.ds(pl.multiple_of(zl * 16, 16), 16), :]
    for dz in (1, 3, 2):
        z_copy(dz).wait_recv()
        acc = acc + zbuf[dz - 1]

    full[core, pl.ds(pl.multiple_of(x * 64 + zl * 16, 16), 16), :] = acc

    def gz_copy(dz, source):
        spot = full.at[core, pl.ds(x * 64 + source * 16, 16), :]
        return rcopy(spot, spot, s_gz.at[dz - 1], r_gz.at[dz - 1], dev_line(dz))

    def gx_copy(dx, source):
        spot = full.at[core, pl.ds(source * 64, 64), :]
        return rcopy(spot, spot, s_gx.at[dx - 1], r_gx.at[dx - 1], dev(dx, 0, 0, 0))

    def gs_copy(dx, half_at):
        spot = full.at[half_at, pl.ds(((x + 4 - dx) % 4) * 64, 64), :]
        return rcopy(spot, spot, s_gs.at[dx], r_gs.at[dx], sibling)

    for dz in (1, 3, 2):
        gz_copy(dz, zl).start()
    for dz in (1, 3, 2):
        gz_copy(dz, (zl + 4 - dz) % 4).wait_recv()
    for dx in (2, 1, 3):
        gx_copy(dx, x).start()
    gs_copy(0, core).start()
    for dx in (1, 3, 2):
        gx_copy(dx, (x + 4 - dx) % 4).wait_recv()
        gs_copy(dx, core).start()
    for dx in (0, 1, 3, 2):
        gs_copy(dx, 1 - core).wait_recv()
    result = pltpu.make_async_copy(full, out, s_out)
    result.start()

    for near in range(8):
        for other in range(2):
            if near or other:
                ingest_copy(near, other).wait_send()
    order_copy.wait_send()
    sib_copy.wait_send()
    for near in range(1, 8):
        red_copy(near).wait_send()
    for dy in range(8):
        for other in range(2):
            if dy or other:
                hint_copy(dy, other).wait_send()
            else:
                @pl.when(jnp.logical_not(local))
                def _():
                    hint_copy(0, 0).wait_send()
    for d in range(1, 4):
        x_copy(d).wait_send()
        z_copy(d).wait_send()
        gz_copy(d, zl).wait_send()
        gx_copy(d, x).wait_send()
    for d in range(4):
        gs_copy(d, core).wait_send()
    result.wait()


def on_device(ingest, row_order, matrix_seeds):
    dma = pltpu.SemaphoreType.DMA
    scratch = [
        pltpu.VMEM((256, 2048), BF16),
        pltpu.VMEM((2, 8, 256), I32),
        pltpu.VMEM((1024, 16), BF16),
        pltpu.VMEM((2, 16, 2048), BF16),
        pltpu.VMEM((1024, 1024), BF16),
        pltpu.VMEM((1024, 1024), BF16),
        pltpu.VMEM((2, 256, 512), I32),
        pltpu.VMEM((256, 512), I32),
        pltpu.VMEM((8, 32, 512), I32),
        pltpu.VMEM((8, 16, 128), I32),
        pltpu.VMEM((256, 128), I32),
        pltpu.VMEM((4, 512, 512), BF16),
        pltpu.VMEM((256, 512), I32),
        pltpu.VMEM((3, 64, 512), I32),
        pltpu.VMEM((64, 512), I32),
        pltpu.VMEM((3, 16, 512), I32),
        pltpu.VMEM((2, 256, 512), I32),
        dma((16,)), dma((16,)), dma, dma, dma, dma, dma((8,)), dma((8,)), dma((16,)), dma((16,)),
        dma((3,)), dma((3,)), dma((3,)), dma((3,)), dma((3,)), dma((3,)), dma((3,)), dma((3,)),
        dma((4,)), dma((4,)), dma,
    ]
    total = pl.pallas_call(
        kernel,
        out_shape=jax.ShapeDtypeStruct((2, 256, 512), I32),
        in_specs=[
            pl.BlockSpec(memory_space=pltpu.SMEM),
            pl.BlockSpec(memory_space=pl.ANY),
            pl.BlockSpec(memory_space=pltpu.VMEM),
        ],
        out_specs=pl.BlockSpec(memory_space=pl.ANY),
        scratch_shapes=scratch,
        compiler_params=pltpu.CompilerParams(
            collective_id=0, has_side_effects=True, vmem_limit_bytes=48 * 2**20
        ),
        name="hints",
    )(matrix_seeds, ingest, row_order)
    total = jnp.transpose(total.reshape(2, 4, 64, 512), (1, 2, 0, 3)).reshape(4, 64, 1024)
    low = (total & 65535).astype(F32)
    high = lax.shift_right_logical(total, jnp.int32(16)).astype(F32)
    return jnp.stack([low, high], axis=1) * (1.0 / 65536.0)


def solution(mesh):
    return jax.shard_map(
        on_device, mesh=mesh,
        in_specs=(P(("row", "col"), None), P("row", None), P()),
        out_specs=P(None, None, "col", None), check_vma=False,
    )
```

```python
import functools

import jax
import jax.numpy as jnp
from jax import lax
from jax.experimental import pallas as pl
from jax.experimental.pallas import tpu as pltpu
from jax.sharding import PartitionSpec as P

PRIME = 46337
HALF = 23168
INV = 1.0 / PRIME
MAGIC_ONE = 1.5 * 2.0**23
MAGIC_BYTE = 1.5 * 2.0**31
BIAS = (HALF * 65537 - 0x80808080) % 2**32
BIAS = BIAS - 2**32 if BIAS >= 2**31 else BIAS
NEAR = ((0, 0, 0), (0, 1, 0), (1, 0, 0), (0, 0, 1), (0, 1, 1), (0, 0, -1), (-1, 0, 0), (0, -1, 0))
ORDER = (4, 1, 2, 3, 5, 6, 7, 0)
MESH = pl.DeviceIdType.MESH
F32, BF16, I32 = jnp.float32, jnp.bfloat16, jnp.int32
NT = (((1,), (1,)), ((), ()))
NN = (((1,), (0,)), ((), ()))


def modp(v):
    q = (v.astype(F32) * INV).astype(I32)
    r = v - q * PRIME
    r = jnp.where(r < 0, r + PRIME, r)
    return jnp.where(r >= PRIME, r - PRIME, r)


def centred(v):
    return jnp.where(v > HALF, v - PRIME, v)


def two_digits(v):
    hi = ((v + 128 + 65536) // 256 - 256) * 256
    return hi, v - hi


def pick_rows(rows, shape):
    at = lax.broadcasted_iota(I32, shape, 0)
    out = jnp.zeros(shape, I32)
    for k, row in enumerate(rows):
        out = jnp.where(at == k, row, out)
    return out.astype(F32)


def index_digits(index, seed):
    x = modp(modp(index * 40503) + seed)
    x = modp(x * x)
    hi, lo = two_digits(centred(modp(x * x)))
    nib = [lax.shift_right_logical(x, jnp.int32(4 * k)) & 15 for k in range(4)]
    one = jnp.ones_like(x)
    return pick_rows(nib + nib + [hi, lo, one, one], (16, index.shape[1]))


def column_digits(index):
    b = modp(index * 29989)
    his, los = [], []
    w = modp(b + b)
    for k in range(4):
        hi, lo = two_digits(centred(w))
        his.append(hi)
        los.append(lo)
        w = modp(w * 16)
    hi, lo = two_digits(centred(modp(modp(b * b) + (12345 - HALF + PRIME))))
    one = jnp.ones_like(b)
    return pick_rows(his + los + [one, one, hi, lo], (16, index.shape[1]))


def residue_digits(v):
    q = (v * INV + MAGIC_ONE) - MAGIC_ONE
    r = v - q * PRIME
    hi = (r + MAGIC_BYTE) - MAGIC_BYTE
    return (r - hi).astype(BF16), hi.astype(BF16)


def joined(parts):
    t = parts[0].astype(I32)
    t = t + lax.shift_left((parts[1] * (1.0 / 256)).astype(I32), jnp.int32(8))
    t = t + lax.shift_left(parts[2].astype(I32), jnp.int32(16))
    return t + lax.shift_left((parts[3] * (1.0 / 256)).astype(I32), jnp.int32(24))


def kernel(
    seeds, ingest, order, out,
    rec, order_in, orders, bdig, xdig, xdig2, gen_a, gen_b, give, sib, mine, red, hint_send, hall, a2,
    tot, tsib, zbuf, full,
    s_in, r_in, s_own, s_ord, r_ord, s_sib, r_sib, s_red, r_red, s_hint, r_hint, s_hx, r_hx, s_tot, r_tot,
    s_z, r_z, s_gz, r_gz, s_gx, r_gx, s_gs, r_gs, s_out,
):
    row, col = lax.axis_index("row"), lax.axis_index("col")
    core, x, zl = row % 2, (row // 2) % 4, row // 8
    y, zh = col % 8, col // 8
    z = zh * 4 + zl

    def dev_at(xx, yy, zz, cc):
        return {"row": ((zz % 4) * 4 + xx) * 2 + cc, "col": (zz // 4) * 8 + yy}

    def dev(dx, dy, dz, other):
        return dev_at((x + dx + 4) % 4, (y + dy + 8) % 8, (z + dz + 8) % 8, (core + other) % 2)

    def dev_line(dz):
        return dev_at(x, y, zh * 4 + (zl + dz) % 4, core)

    def rcopy(src, dst, ssem, rsem, device):
        return pltpu.make_async_remote_copy(
            src_ref=src, dst_ref=dst, send_sem=ssem, recv_sem=rsem, device_id=device, device_id_type=MESH
        )

    sibling = dev(0, 0, 0, 1)

    def arrived(spot, rsem):
        rcopy(spot, spot, s_tot, rsem, sibling).wait_recv()

    order_load = pltpu.make_async_copy(order, order_in, s_own)
    order_load.start()

    barrier = pltpu.get_barrier_semaphore()

    def greet(device):
        pl.semaphore_signal(barrier, inc=1, device_id=device, device_id_type=MESH)

    def greet_plane(k, carry):
        side = k // 16
        zz = z + side * (7 - 2 * z)
        greet(dev_at(x, (y + (k // 2) % 8) % 8, zz, (core + k) % 2))
        return carry

    lax.fori_loop(1, 32, greet_plane, 0)
    count = 31
    for off in ((1, 0, 0), (-1, 0, 0), (0, 0, 1), (0, 0, -1), (0, 1, 1), (0, -1, -1)):
        for other in range(2):
            greet(dev(*off, other))
            count += 1
    greet(dev(2, 0, 0, 0))
    for d in range(1, 4):
        greet(dev_line(d))
        greet(dev_at((x + d) % 4, y, 7 - z, core))
    pl.semaphore_wait(barrier, count + 7)

    colour = (2 * x + y + 3 * z) % 8
    sign = 1 - 2 * core

    def ingest_src(near, other):
        return ingest.at[:, pl.ds(((colour + near) % 8) * 4096 + ((core + other) % 2) * 2048, 2048)]

    def ingest_copy(near, other):
        slot = near * 2 + core
        device = dev(0, sign, sign, other) if near == 4 else dev(*NEAR[near], other)
        return rcopy(
            ingest_src(near, other), rec.at[pl.ds(slot * 16, 16), :],
            s_in.at[near * 2 + other], r_in.at[slot], device,
        )

    for near in ORDER:
        for other in range(2):
            if near or other:
                ingest_copy(near, other).start()
    own_in = pltpu.make_async_copy(ingest_src(0, 0), rec.at[pl.ds(core * 16, 16), :], r_in.at[core])
    own_in.start()

    order_load.wait()
    orders[0, 0] = jnp.broadcast_to(order_in[...], (8, 256))

    def order_copy(k):
        side, dx = k // 4, k % 4
        zz = 7 - z if side else z
        return rcopy(
            orders.at[0, 0], orders.at[side, dx], s_ord.at[k], r_ord.at[k], dev_at((x + dx) % 4, y, zz, core)
        )

    for k in range(1, 8):
        order_copy(k).start()

    bdig[...] = jnp.transpose(column_digits(lax.broadcasted_iota(I32, (1, 1024), 1))).astype(BF16)
    lane = lax.broadcasted_iota(I32, (1, 2048), 1)
    mirrored = (lane // 256) % 2
    block = ((zl + mirrored * (3 - 2 * zl)) * 4 + (x + 4 - lane // 512) % 4) * 2 + core
    for w in range(2):
        xdig[w] = index_digits(lane + (colour * 4096 + core * 2048), seeds[0] + 7919 * w).astype(BF16)
        xdig2[w] = index_digits(block * 256 + lane % 256, seeds[1] + 7919 * w).astype(BF16)

    def generate(buf, t, kh):
        n_at = pl.multiple_of((((1 - core) * 2 + t) % 4) * 256, 256)
        left = bdig[pl.ds(n_at, 256), :]
        for w in range(2):
            digits = xdig[w, :, kh * 1024 : (kh + 1) * 1024]
            lo, hi = residue_digits(lax.dot_general(left, digits, NN, preferred_element_type=F32))
            buf[(2 * w) * 256 : (2 * w + 1) * 256, :] = lo
            buf[(2 * w + 1) * 256 : (2 * w + 2) * 256, :] = hi

    def multiply(buf, kh):
        r = lax.dot_general(buf[...], rec[:, kh * 1024 : (kh + 1) * 1024], NT, preferred_element_type=F32)
        return joined([r[k * 256 : (k + 1) * 256, :] for k in range(4)])

    def ahead(t, carry):
        for kh in range(2):
            generate(gen_a.at[t * 2 + kh], t, kh)
        return carry

    lax.fori_loop(0, 2, ahead, 0)

    for k in range(1, 8):
        arrived(orders.at[k // 4, k % 4], r_ord.at[k])
    spot = lax.broadcasted_iota(I32, (256, 1), 0)
    side = (spot // 64) % 2
    ingest_row = ((zh + side * (1 - 2 * zh)) * 8 + (spot // 8) % 8) * 16 + (spot // 128) * 8 + spot % 8
    wanted = ingest_row + 256 * side
    lane = lax.broadcasted_iota(I32, (1, 512), 1)
    quarter = bdig[pl.ds(pl.multiple_of(x * 256, 256), 256), :]
    for dx in range(4):
        have = jnp.concatenate([orders[0, dx, 0:1, :], orders[1, dx, 0:1, :]], axis=1) + (lane // 256) * 256
        onehot = (wanted == have).astype(F32).astype(BF16)
        for w in range(2):
            digits = xdig2[w, :, dx * 512 : (dx + 1) * 512]
            perm = lax.dot_general(onehot, digits, NT, preferred_element_type=F32).astype(BF16)
            lo, hi = residue_digits(lax.dot_general(perm, quarter, NT, preferred_element_type=F32))
            a2[2 * w, dx * 256 : (dx + 1) * 256, :] = lo
            a2[2 * w + 1, dx * 256 : (dx + 1) * 256, :] = hi

    for slot in range(16):
        arrived(rec.at[pl.ds(slot * 16, 16), :], r_in.at[slot])
    sums = lax.dot_general(jnp.ones((16, 2048), BF16), rec[...], NT, preferred_element_type=F32)
    bias = sums[0:1, :].astype(I32) * jnp.int32(BIAS)

    def tile(t, carry):
        acc = bias
        for kh in range(2):
            generate(gen_b.at[t * 2 + kh], t + 2, kh)
            acc = acc + multiply(gen_a.at[t * 2 + kh], kh)
        give[t] = jnp.transpose(acc)
        return carry

    lax.fori_loop(0, 2, tile, 0)
    sib_copy = rcopy(give, sib, s_sib, r_sib, sibling)
    sib_copy.start()

    def red_copy(q, near):
        if near in (4, 8):
            at, sg = (near // 4 - 1) * 16, 1 if near == 8 else -1
            rows, dst, device = 128 + at, red.at[q, 4, pl.ds(at, 16), :], dev(0, sg, sg, 0)
            rows = mine.at[q, pl.ds(rows, 16), :]
        else:
            dx, dy, dz = NEAR[near]
            rows, dst, device = mine.at[q, pl.ds(near * 32, 32), :], red.at[q, near], dev(-dx, -dy, -dz, 0)
        return rcopy(rows, dst, s_red.at[q * 9 + near], r_red.at[q * 9 + near], device)

    for q in range(2):
        acc = bias
        for kh in range(2):
            acc = acc + multiply(gen_b.at[q * 2 + kh], kh)
        acc = jnp.transpose(acc)
        if q == 0:
            sib_copy.wait_recv()
        mine[q] = acc + sib[q]
        for near in (4, 8, 1, 2, 3, 5, 6, 7):
            red_copy(q, near).start()
    hints = []
    for q in range(2):
        hint = mine[q, 0:32, :]
        for near in (1, 2, 3, 5, 6, 7, 4, 8):
            red_copy(q, near).wait_recv()
        for near in range(1, 8):
            hint = hint + red[q, near]
        hints.append(hint)

    low_lane = lax.broadcasted_iota(I32, (8, 128), 1) < 64
    for t in range(4):
        for cc in range(2):
            tile_at = hints[t // 2][cc * 16 : (cc + 1) * 16, (t % 2) * 128 : (t % 2 + 1) * 128]
            top, low = tile_at[0:8, :], tile_at[8:16, :]
            hint_send[2 * t, cc] = jnp.where(low_lane, top, pltpu.roll(low, 64, 1))
            hint_send[2 * t + 1, cc] = jnp.where(low_lane, pltpu.roll(top, 64, 1), low)
    away = (zh + core) % 2
    local = away == 0
    landing = hall.at[0, pl.ds((away * 8 + y) * 8, 8), :]
    landed = r_hint.at[away * 8 + y]

    def hint_copy(dy, other):
        yy = (y + dy) % 8
        return rcopy(
            hint_send.at[yy, (core + other) % 2], landing, s_hint.at[dy * 2 + other], landed,
            dev_at(x, yy, z + away * (7 - 2 * z), (core + other) % 2),
        )

    own_hint = pltpu.make_async_copy(hint_send.at[y, core], landing, landed)
    for dy in (4, 3, 5, 2, 6, 1, 7, 0):
        for other in range(2):
            if dy or other:
                hint_copy(dy, other).start()
            else:
                @pl.when(local)
                def _():
                    own_hint.start()

                @pl.when(jnp.logical_not(local))
                def _():
                    hint_copy(0, 0).start()

    for k in range(16):
        arrived(hall.at[0, pl.ds(k * 8, 8), :], r_hint.at[k])

    def hx_copy(k):
        if k < 2:
            return rcopy(hall.at[0], hall.at[1 + 2 * k], s_hx.at[k], r_hx.at[k], dev(1 - 2 * k, 0, 0, 0))
        at = pl.ds((k - 2) * 64, 64)
        return rcopy(
            hall.at[2 * k - 3, at, :], hall.at[2, at, :], s_hx.at[k], r_hx.at[k], dev(5 - 2 * k, 0, 0, 0)
        )

    for k in range(2):
        hx_copy(k).start()

    def second(dx, total):
        turned = jnp.transpose(hall[dx])
        wide = jnp.concatenate([turned[0:64, :], turned[64:128, :]], axis=1)
        left = jnp.concatenate(
            [
                ((lax.shift_right_logical(wide, jnp.int32(8 * d)) & 255) - 128).astype(F32).astype(BF16)
                for d in range(4)
            ],
            axis=0,
        )
        lsum = lax.dot_general(left, jnp.ones((256, 128), BF16), NN, preferred_element_type=F32)
        term = joined(
            [
                lax.dot_general(left, a2[k, dx * 256 : (dx + 1) * 256, :], NN, preferred_element_type=F32)
                for k in range(4)
            ]
        )
        term = term + lsum[:, 0:1].astype(I32) * jnp.int32(BIAS)
        return term if total is None else total + term

    total = second(0, None)
    hx_copy(0).wait_recv()
    hx_copy(2).start()
    hx_copy(1).wait_recv()
    hx_copy(3).start()
    total = second(1, total)
    total = second(3, total)
    hx_copy(2).wait_recv()
    hx_copy(3).wait_recv()
    total = second(2, total)
    tot[0] = total[:, 0:128]
    tot[1] = total[:, 128:256]

    tot_copy = rcopy(tot.at[1 - core], tsib.at[0], s_tot, r_tot, sibling)
    tot_copy.start()
    tot_copy.wait_recv()
    tsib[1] = tot[core] + tsib[0]

    def z_copy(dz):
        zz = (zl + dz) % 4
        return rcopy(
            tsib.at[1, pl.ds(zz * 64, 64), :], zbuf.at[dz - 1], s_z.at[dz - 1], r_z.at[dz - 1], dev_line(dz)
        )

    for dz in (1, 3, 2):
        z_copy(dz).start()
    acc = tsib[1, pl.ds(pl.multiple_of(zl * 64, 64), 64), :]
    for dz in (1, 3, 2):
        z_copy(dz).wait_recv()
        acc = acc + zbuf[dz - 1]
    full[x, core, pl.ds(pl.multiple_of(zl * 64, 64), 64), :] = acc

    def part_of(dx, j, cc):
        return full.at[(x + 4 - dx) % 4, cc, pl.ds(((zl + 4 - j) % 4) * 64, 64), :]

    def half_of(dx, j, k):
        return full.at[(x + 4 - dx) % 4, core, pl.ds(((zl + 4 - j) % 4) * 64 + k * 32, 32), :]

    def gz_copy(dz):
        return rcopy(part_of(0, 0, core), part_of(0, 0, core), s_gz.at[dz - 1], r_gz.at[dz - 1], dev_line(dz))

    def gx_copy(j, k):
        spot = part_of(0, j, core) if k < 2 else half_of(2 * k - 3, j, k - 2)
        step = 1 - 2 * (k % 2)
        return rcopy(spot, spot, s_gx.at[j * 4 + k], r_gx.at[j * 4 + k], dev(step, 0, 0, 0))

    def gs_copy(dx, j):
        spot = part_of(dx, j, core)
        return rcopy(spot, spot, s_gs.at[dx * 4 + j], r_gs.at[dx * 4 + j], sibling)

    def out_copy(dx, cc):
        xx = (x + 4 - dx) % 4
        who = (core + cc) % 2
        return pltpu.make_async_copy(
            full.at[xx, who], out.at[:, pl.ds(xx * 256 + who * 128, 128)], s_out.at[dx * 2 + cc]
        )

    def spread(j):
        gx_copy(j, 0).start()
        gx_copy(j, 1).start()
        gs_copy(0, j).start()

    def forward(j):
        arrived(part_of(1, j, core), r_gx.at[j * 4])
        gx_copy(j, 2).start()
        gs_copy(1, j).start()
        arrived(part_of(3, j, core), r_gx.at[j * 4 + 1])
        gx_copy(j, 3).start()
        gs_copy(3, j).start()

    def finish(j):
        arrived(half_of(2, j, 0), r_gx.at[j * 4 + 2])
        arrived(half_of(2, j, 1), r_gx.at[j * 4 + 3])
        gs_copy(2, j).start()

    for dz in (2, 1, 3):
        gz_copy(dz).start()
    spread(0)
    arrived(part_of(0, 1, core), r_gz.at[0])
    spread(1)
    arrived(part_of(0, 3, core), r_gz.at[2])
    spread(3)
    forward(0)
    arrived(part_of(0, 2, core), r_gz.at[1])
    spread(2)
    out_copy(0, 0).start()
    for j in (1, 3, 2):
        forward(j)
    for dx in (1, 3):
        out_copy(dx, 0).start()
    for j in (0, 1, 3, 2):
        finish(j)
    out_copy(2, 0).start()
    for dx in (0, 1, 3, 2):
        for j in (0, 1, 3, 2):
            arrived(part_of(dx, j, 1 - core), r_gs.at[dx * 4 + j])
        out_copy(dx, 1).start()

    for near in range(8):
        for other in range(2):
            if near or other:
                ingest_copy(near, other).wait_send()
    for k in range(1, 8):
        order_copy(k).wait_send()
    sib_copy.wait_send()
    for q in range(2):
        for near in range(1, 9):
            red_copy(q, near).wait_send()
    for dy in range(8):
        for other in range(2):
            if dy or other:
                hint_copy(dy, other).wait_send()
            else:
                @pl.when(jnp.logical_not(local))
                def _():
                    hint_copy(0, 0).wait_send()
    for k in range(4):
        hx_copy(k).wait_send()
    tot_copy.wait_send()
    for d in range(1, 4):
        z_copy(d).wait_send()
        gz_copy(d).wait_send()
    for j in range(4):
        for k in range(4):
            gx_copy(j, k).wait_send()
            gs_copy(k, j).wait_send()
    for dx in range(4):
        for cc in range(2):
            out_copy(dx, cc).wait()


def on_device(ingest, row_order, matrix_seeds):
    dma = pltpu.SemaphoreType.DMA
    scratch = [
        pltpu.VMEM((256, 2048), BF16),
        pltpu.VMEM((1, 256), I32),
        pltpu.VMEM((2, 4, 8, 256), I32),
        pltpu.VMEM((1024, 16), BF16),
        pltpu.VMEM((2, 16, 2048), BF16),
        pltpu.VMEM((2, 16, 2048), BF16),
        pltpu.VMEM((4, 1024, 1024), BF16),
        pltpu.VMEM((4, 1024, 1024), BF16),
        pltpu.VMEM((2, 256, 256), I32),
        pltpu.VMEM((2, 256, 256), I32),
        pltpu.VMEM((2, 256, 256), I32),
        pltpu.VMEM((2, 8, 32, 256), I32),
        pltpu.VMEM((8, 2, 8, 128), I32),
        pltpu.VMEM((4, 128, 128), I32),
        pltpu.VMEM((4, 1024, 256), BF16),
        pltpu.VMEM((2, 256, 128), I32),
        pltpu.VMEM((2, 256, 128), I32),
        pltpu.VMEM((3, 64, 128), I32),
        pltpu.VMEM((4, 2, 256, 128), I32),
        dma((16,)), dma((16,)), dma, dma((8,)), dma((8,)), dma, dma, dma((18,)), dma((18,)), dma((16,)), dma((16,)),
        dma((4,)), dma((4,)), dma, dma, dma((3,)), dma((3,)), dma((3,)), dma((3,)), dma((16,)), dma((16,)),
        dma((16,)), dma((16,)), dma((8,)),
    ]
    total = pl.pallas_call(
        kernel,
        out_shape=jax.ShapeDtypeStruct((256, 1024), I32),
        in_specs=[
            pl.BlockSpec(memory_space=pltpu.SMEM),
            pl.BlockSpec(memory_space=pltpu.HBM),
            pl.BlockSpec(memory_space=pltpu.HBM),
        ],
        out_specs=pl.BlockSpec(memory_space=pltpu.HBM),
        scratch_shapes=scratch,
        compiler_params=pltpu.CompilerParams(
            collective_id=0, has_side_effects=True, vmem_limit_bytes=60 * 2**20
        ),
        name="hints",
    )(matrix_seeds, ingest, row_order)
    shape = (4, 2, 64, 1024)
    shift = lax.broadcasted_iota(I32, shape, 1) * 16
    halves = lax.shift_right_logical(jnp.broadcast_to(total.reshape(4, 1, 64, 1024), shape), shift) & 65535
    return halves.astype(F32) * (1.0 / 65536.0)


def solution(mesh):
    return jax.shard_map(
        on_device, mesh=mesh,
        in_specs=(P(("row", "col"), None), P("row", None), P()),
        out_specs=P(None, None, "col", None), check_vma=False,
    )
```

```python
import functools

import jax
import jax.numpy as jnp
from jax import lax
from jax.experimental import pallas as pl
from jax.experimental.pallas import tpu as pltpu
from jax.sharding import PartitionSpec as P

PRIME = 46337
HALF = 23168
INV = 1.0 / PRIME
MAGIC_ONE = 1.5 * 2.0**23
MAGIC_BYTE = 1.5 * 2.0**31
BIAS = (HALF * 65537 - 0x80808080) % 2**32
BIAS = BIAS - 2**32 if BIAS >= 2**31 else BIAS
NEAR = ((0, 0, 0), (0, 1, 0), (1, 0, 0), (0, 0, 1), (0, 1, 1), (0, 0, -1), (-1, 0, 0), (0, -1, 0))
ORDER = (4, 1, 2, 3, 5, 6, 7, 0)
MESH = pl.DeviceIdType.MESH
F32, BF16, I32 = jnp.float32, jnp.bfloat16, jnp.int32
NT = (((1,), (1,)), ((), ()))
NN = (((1,), (0,)), ((), ()))


def modp(v):
    q = (v.astype(F32) * INV).astype(I32)
    r = v - q * PRIME
    r = jnp.where(r < 0, r + PRIME, r)
    return jnp.where(r >= PRIME, r - PRIME, r)


def centred(v):
    return jnp.where(v > HALF, v - PRIME, v)


def two_digits(v):
    hi = ((v + 128 + 65536) // 256 - 256) * 256
    return hi, v - hi


def pick_rows(rows, shape):
    at = lax.broadcasted_iota(I32, shape, 0)
    out = jnp.zeros(shape, I32)
    for k, row in enumerate(rows):
        out = jnp.where(at == k, row, out)
    return out.astype(F32)


def index_digits(index, seed):
    x = modp(modp(index * 40503) + seed)
    x = modp(x * x)
    hi, lo = two_digits(centred(modp(x * x)))
    nib = [lax.shift_right_logical(x, jnp.int32(4 * k)) & 15 for k in range(4)]
    one = jnp.ones_like(x)
    return pick_rows(nib + nib + [hi, lo, one, one], (16, index.shape[1]))


def column_digits(index):
    b = modp(index * 29989)
    his, los = [], []
    w = modp(b + b)
    for k in range(4):
        hi, lo = two_digits(centred(w))
        his.append(hi)
        los.append(lo)
        w = modp(w * 16)
    hi, lo = two_digits(centred(modp(modp(b * b) + (12345 - HALF + PRIME))))
    one = jnp.ones_like(b)
    return pick_rows(his + los + [one, one, hi, lo], (16, index.shape[1]))


def residue_digits(v):
    q = (v * INV + MAGIC_ONE) - MAGIC_ONE
    r = v - q * PRIME
    hi = (r + MAGIC_BYTE) - MAGIC_BYTE
    return (r - hi).astype(BF16), hi.astype(BF16)


def joined(parts):
    t = parts[0].astype(I32)
    t = t + lax.shift_left((parts[1] * (1.0 / 256)).astype(I32), jnp.int32(8))
    t = t + lax.shift_left(parts[2].astype(I32), jnp.int32(16))
    return t + lax.shift_left((parts[3] * (1.0 / 256)).astype(I32), jnp.int32(24))


def kernel(
    seeds, ingest, order, out,
    rec, order_in, orders, bdig, xdig, xdig2, gen_a, gen_b, give, sib, mine, red, hint_send, hall, a2,
    tot, tsib, zbuf, full, known,
    s_in, r_in, s_own, s_ord, r_ord, s_sib, r_sib, s_red, r_red, s_hint, r_hint, s_hx, r_hx, s_tot, r_tot,
    s_z, r_z, s_gz, r_gz, s_gx, r_gx, s_gs, r_gs, s_out,
):
    row, col = lax.axis_index("row"), lax.axis_index("col")
    core, x, zl = row % 2, (row // 2) % 4, row // 8
    y, zh = col % 8, col // 8
    z = zh * 4 + zl

    def dev_at(xx, yy, zz, cc):
        return {"row": ((zz % 4) * 4 + xx) * 2 + cc, "col": (zz // 4) * 8 + yy}

    def dev(dx, dy, dz, other):
        return dev_at((x + dx + 4) % 4, (y + dy + 8) % 8, (z + dz + 8) % 8, (core + other) % 2)

    def dev_line(dz):
        return dev_at(x, y, zh * 4 + (zl + dz) % 4, core)

    def rcopy(src, dst, ssem, rsem, device):
        return pltpu.make_async_remote_copy(
            src_ref=src, dst_ref=dst, send_sem=ssem, recv_sem=rsem, device_id=device, device_id_type=MESH
        )

    sibling = dev(0, 0, 0, 1)

    def arrived(spot, rsem):
        rcopy(spot, spot, s_tot, rsem, sibling).wait_recv()

    order_load = pltpu.make_async_copy(order, order_in, s_own)
    order_load.start()

    barrier = pltpu.get_barrier_semaphore()

    def greet(device, sem):
        pl.semaphore_signal(sem, inc=1, device_id=device, device_id_type=MESH)

    count = 1
    greet(sibling, barrier)
    for off in ((0, 1, 0), (0, -1, 0), (1, 0, 0), (-1, 0, 0), (0, 0, 1), (0, 0, -1), (0, 1, 1), (0, -1, -1)):
        for other in range(2):
            greet(dev(*off, other), barrier)
            count += 1
    pl.semaphore_wait(barrier, count)

    def round_send(k):
        dx, dy, dz = ((1, 0, 0), (0, 1, 0), (0, 2, 0), (0, 0, 1), (0, 0, 2))[k]
        greet(dev(dx, dy, dz, 0), known.at[k])
        greet(dev(-dx, -dy, -dz, 0), known.at[k])

    def round_wait(k):
        pl.semaphore_wait(known.at[k], 2)

    colour = (2 * x + y + 3 * z) % 8
    sign = 1 - 2 * core

    def ingest_src(near, other):
        return ingest.at[:, pl.ds(((colour + near) % 8) * 4096 + ((core + other) % 2) * 2048, 2048)]

    def ingest_copy(near, other):
        slot = near * 2 + core
        device = dev(0, sign, sign, other) if near == 4 else dev(*NEAR[near], other)
        return rcopy(
            ingest_src(near, other), rec.at[pl.ds(slot * 16, 16), :],
            s_in.at[near * 2 + other], r_in.at[slot], device,
        )

    for near in ORDER:
        for other in range(2):
            if near or other:
                ingest_copy(near, other).start()
    own_in = pltpu.make_async_copy(ingest_src(0, 0), rec.at[pl.ds(core * 16, 16), :], r_in.at[core])
    own_in.start()
    round_send(0)

    bdig[...] = jnp.transpose(column_digits(lax.broadcasted_iota(I32, (1, 1024), 1))).astype(BF16)
    index = lax.broadcasted_iota(I32, (1, 2048), 1) + (colour * 4096 + core * 2048)
    for w in range(2):
        xdig[w] = index_digits(index, seeds[0] + 7919 * w).astype(BF16)
    round_wait(0)
    round_send(1)

    def generate(buf, t, kh):
        n_at = pl.multiple_of((((1 - core) * 2 + t) % 4) * 256, 256)
        left = bdig[pl.ds(n_at, 256), :]
        for w in range(2):
            digits = xdig[w, :, kh * 1024 : (kh + 1) * 1024]
            lo, hi = residue_digits(lax.dot_general(left, digits, NN, preferred_element_type=F32))
            buf[(2 * w) * 256 : (2 * w + 1) * 256, :] = lo
            buf[(2 * w + 1) * 256 : (2 * w + 2) * 256, :] = hi

    def multiply(buf, kh):
        r = lax.dot_general(buf[...], rec[:, kh * 1024 : (kh + 1) * 1024], NT, preferred_element_type=F32)
        return joined([r[k * 256 : (k + 1) * 256, :] for k in range(4)])

    for kh in range(2):
        generate(gen_a.at[kh], 0, kh)
    round_wait(1)
    round_send(2)

    for slot in range(16):
        arrived(rec.at[pl.ds(slot * 16, 16), :], r_in.at[slot])
    sums = lax.dot_general(jnp.ones((16, 2048), BF16), rec[...], NT, preferred_element_type=F32)
    bias = sums[0:1, :].astype(I32) * jnp.int32(BIAS)

    gens = (gen_a, gen_b)

    def tile(t):
        acc = bias
        for kh in range(2):
            if t < 3:
                generate(gens[(t + 1) % 2].at[kh], t + 1, kh)
            acc = acc + multiply(gens[t % 2].at[kh], kh)
        return jnp.transpose(acc)

    round_wait(2)
    round_send(3)
    give[0] = tile(0)
    round_wait(3)
    round_send(4)
    give[1] = tile(1)
    round_wait(4)
    sib_copy = rcopy(give, sib, s_sib, r_sib, sibling)
    sib_copy.start()

    order_load.wait()
    orders[0, 0] = jnp.broadcast_to(order_in[...], (8, 256))

    def order_copy(k):
        side, dx = k // 4, k % 4
        zz = 7 - z if side else z
        return rcopy(
            orders.at[0, 0], orders.at[side, dx], s_ord.at[k], r_ord.at[k], dev_at((x + dx) % 4, y, zz, core)
        )

    for k in range(1, 8):
        order_copy(k).start()

    def red_copy(q, near):
        if near in (4, 8):
            at, sg = (near // 4 - 1) * 16, 1 if near == 8 else -1
            rows, dst, device = 128 + at, red.at[q, 4, pl.ds(at, 16), :], dev(0, sg, sg, 0)
            rows = mine.at[q, pl.ds(rows, 16), :]
        else:
            dx, dy, dz = NEAR[near]
            rows, dst, device = mine.at[q, pl.ds(near * 32, 32), :], red.at[q, near], dev(-dx, -dy, -dz, 0)
        return rcopy(rows, dst, s_red.at[q * 9 + near], r_red.at[q * 9 + near], device)

    for q in range(2):
        acc = tile(2 + q)
        if q == 0:
            sib_copy.wait_recv()
        mine[q] = acc + sib[q]
        for near in (4, 8, 1, 2, 3, 5, 6, 7):
            red_copy(q, near).start()
    lane = lax.broadcasted_iota(I32, (1, 2048), 1)
    mirrored = (lane // 256) % 2
    block = ((zl + mirrored * (3 - 2 * zl)) * 4 + (x + 4 - lane // 512) % 4) * 2 + core
    for w in range(2):
        xdig2[w] = index_digits(block * 256 + lane % 256, seeds[1] + 7919 * w).astype(BF16)

    for k in range(1, 8):
        arrived(orders.at[k // 4, k % 4], r_ord.at[k])
    spot = lax.broadcasted_iota(I32, (256, 1), 0)
    side = (spot // 64) % 2
    ingest_row = ((zh + side * (1 - 2 * zh)) * 8 + (spot // 8) % 8) * 16 + (spot // 128) * 8 + spot % 8
    wanted = ingest_row + 256 * side
    lane = lax.broadcasted_iota(I32, (1, 512), 1)
    quarter = bdig[pl.ds(pl.multiple_of(x * 256, 256), 256), :]
    for dx in range(4):
        have = jnp.concatenate([orders[0, dx, 0:1, :], orders[1, dx, 0:1, :]], axis=1) + (lane // 256) * 256
        onehot = (wanted == have).astype(F32).astype(BF16)
        for w in range(2):
            digits = xdig2[w, :, dx * 512 : (dx + 1) * 512]
            perm = lax.dot_general(onehot, digits, NT, preferred_element_type=F32).astype(BF16)
            lo, hi = residue_digits(lax.dot_general(perm, quarter, NT, preferred_element_type=F32))
            a2[2 * w, dx * 256 : (dx + 1) * 256, :] = lo
            a2[2 * w + 1, dx * 256 : (dx + 1) * 256, :] = hi

    hints = []
    for q in range(2):
        hint = mine[q, 0:32, :]
        for near in (1, 2, 3, 5, 6, 7, 4, 8):
            red_copy(q, near).wait_recv()
        for near in range(1, 8):
            hint = hint + red[q, near]
        hints.append(hint)

    low_lane = lax.broadcasted_iota(I32, (8, 128), 1) < 64
    for t in range(4):
        for cc in range(2):
            tile_at = hints[t // 2][cc * 16 : (cc + 1) * 16, (t % 2) * 128 : (t % 2 + 1) * 128]
            top, low = tile_at[0:8, :], tile_at[8:16, :]
            hint_send[2 * t, cc] = jnp.where(low_lane, top, pltpu.roll(low, 64, 1))
            hint_send[2 * t + 1, cc] = jnp.where(low_lane, pltpu.roll(top, 64, 1), low)
    away = (zh + core) % 2
    local = away == 0
    landing = hall.at[0, pl.ds((away * 8 + y) * 8, 8), :]
    landed = r_hint.at[away * 8 + y]

    def hint_copy(dy, other):
        yy = (y + dy) % 8
        return rcopy(
            hint_send.at[yy, (core + other) % 2], landing, s_hint.at[dy * 2 + other], landed,
            dev_at(x, yy, z + away * (7 - 2 * z), (core + other) % 2),
        )

    own_hint = pltpu.make_async_copy(hint_send.at[y, core], landing, landed)
    for dy in (4, 3, 5, 2, 6, 1, 7, 0):
        for other in range(2):
            if dy or other:
                hint_copy(dy, other).start()
            else:
                @pl.when(local)
                def _():
                    own_hint.start()

                @pl.when(jnp.logical_not(local))
                def _():
                    hint_copy(0, 0).start()

    for k in range(16):
        arrived(hall.at[0, pl.ds(k * 8, 8), :], r_hint.at[k])

    def hx_copy(k):
        if k < 2:
            return rcopy(hall.at[0], hall.at[1 + 2 * k], s_hx.at[k], r_hx.at[k], dev(1 - 2 * k, 0, 0, 0))
        at = pl.ds((k - 2) * 64, 64)
        return rcopy(
            hall.at[2 * k - 3, at, :], hall.at[2, at, :], s_hx.at[k], r_hx.at[k], dev(5 - 2 * k, 0, 0, 0)
        )

    for k in range(2):
        hx_copy(k).start()

    def second(dx, total):
        turned = jnp.transpose(hall[dx])
        wide = jnp.concatenate([turned[0:64, :], turned[64:128, :]], axis=1)
        left = jnp.concatenate(
            [
                ((lax.shift_right_logical(wide, jnp.int32(8 * d)) & 255) - 128).astype(F32).astype(BF16)
                for d in range(4)
            ],
            axis=0,
        )
        lsum = lax.dot_general(left, jnp.ones((256, 128), BF16), NN, preferred_element_type=F32)
        term = joined(
            [
                lax.dot_general(left, a2[k, dx * 256 : (dx + 1) * 256, :], NN, preferred_element_type=F32)
                for k in range(4)
            ]
        )
        term = term + lsum[:, 0:1].astype(I32) * jnp.int32(BIAS)
        return term if total is None else total + term

    total = second(0, None)
    hx_copy(0).wait_recv()
    hx_copy(2).start()
    hx_copy(1).wait_recv()
    hx_copy(3).start()
    total = second(1, total)
    total = second(3, total)
    hx_copy(2).wait_recv()
    hx_copy(3).wait_recv()
    total = second(2, total)
    tot[0] = total[:, 0:128]
    tot[1] = total[:, 128:256]

    tot_copy = rcopy(tot.at[1 - core], tsib.at[0], s_tot, r_tot, sibling)
    tot_copy.start()
    tot_copy.wait_recv()
    tsib[1] = tot[core] + tsib[0]

    def z_copy(dz):
        zz = (zl + dz) % 4
        return rcopy(
            tsib.at[1, pl.ds(zz * 64, 64), :], zbuf.at[dz - 1], s_z.at[dz - 1], r_z.at[dz - 1], dev_line(dz)
        )

    for dz in (1, 3, 2):
        z_copy(dz).start()
    acc = tsib[1, pl.ds(pl.multiple_of(zl * 64, 64), 64), :]
    for dz in (1, 3, 2):
        z_copy(dz).wait_recv()
        acc = acc + zbuf[dz - 1]
    full[x, core, pl.ds(pl.multiple_of(zl * 64, 64), 64), :] = acc

    def part_of(dx, j, cc):
        return full.at[(x + 4 - dx) % 4, cc, pl.ds(((zl + 4 - j) % 4) * 64, 64), :]

    def half_of(dx, j, k):
        return full.at[(x + 4 - dx) % 4, core, pl.ds(((zl + 4 - j) % 4) * 64 + k * 32, 32), :]

    def gz_copy(dz):
        return rcopy(part_of(0, 0, core), part_of(0, 0, core), s_gz.at[dz - 1], r_gz.at[dz - 1], dev_line(dz))

    def gx_copy(j, k):
        spot = part_of(0, j, core) if k < 2 else half_of(2 * k - 3, j, k - 2)
        step = 1 - 2 * (k % 2)
        return rcopy(spot, spot, s_gx.at[j * 4 + k], r_gx.at[j * 4 + k], dev(step, 0, 0, 0))

    def gs_copy(dx, j):
        spot = part_of(dx, j, core)
        return rcopy(spot, spot, s_gs.at[dx * 4 + j], r_gs.at[dx * 4 + j], sibling)

    def out_copy(dx, cc):
        xx = (x + 4 - dx) % 4
        who = (core + cc) % 2
        return pltpu.make_async_copy(
            full.at[xx, who], out.at[:, pl.ds(xx * 256 + who * 128, 128)], s_out.at[dx * 2 + cc]
        )

    def spread(j):
        gx_copy(j, 0).start()
        gx_copy(j, 1).start()
        gs_copy(0, j).start()

    def forward(j):
        arrived(part_of(1, j, core), r_gx.at[j * 4])
        gx_copy(j, 2).start()
        gs_copy(1, j).start()
        arrived(part_of(3, j, core), r_gx.at[j * 4 + 1])
        gx_copy(j, 3).start()
        gs_copy(3, j).start()

    def finish(j):
        arrived(half_of(2, j, 0), r_gx.at[j * 4 + 2])
        arrived(half_of(2, j, 1), r_gx.at[j * 4 + 3])
        gs_copy(2, j).start()

    for dz in (2, 1, 3):
        gz_copy(dz).start()
    spread(0)
    arrived(part_of(0, 1, core), r_gz.at[0])
    spread(1)
    arrived(part_of(0, 3, core), r_gz.at[2])
    spread(3)
    forward(0)
    arrived(part_of(0, 2, core), r_gz.at[1])
    spread(2)
    out_copy(0, 0).start()
    for j in (1, 3, 2):
        forward(j)
    for dx in (1, 3):
        out_copy(dx, 0).start()
    for j in (0, 1, 3, 2):
        finish(j)
    out_copy(2, 0).start()
    for dx in (0, 1, 3, 2):
        for j in (0, 1, 3, 2):
            arrived(part_of(dx, j, 1 - core), r_gs.at[dx * 4 + j])
        out_copy(dx, 1).start()

    for near in range(8):
        for other in range(2):
            if near or other:
                ingest_copy(near, other).wait_send()
    for k in range(1, 8):
        order_copy(k).wait_send()
    sib_copy.wait_send()
    for q in range(2):
        for near in range(1, 9):
            red_copy(q, near).wait_send()
    for dy in range(8):
        for other in range(2):
            if dy or other:
                hint_copy(dy, other).wait_send()
            else:
                @pl.when(jnp.logical_not(local))
                def _():
                    hint_copy(0, 0).wait_send()
    for k in range(4):
        hx_copy(k).wait_send()
    tot_copy.wait_send()
    for d in range(1, 4):
        z_copy(d).wait_send()
        gz_copy(d).wait_send()
    for j in range(4):
        for k in range(4):
            gx_copy(j, k).wait_send()
            gs_copy(k, j).wait_send()
    for dx in range(4):
        for cc in range(2):
            out_copy(dx, cc).wait()


def on_device(ingest, row_order, matrix_seeds):
    dma = pltpu.SemaphoreType.DMA
    scratch = [
        pltpu.VMEM((256, 2048), BF16),
        pltpu.VMEM((1, 256), I32),
        pltpu.VMEM((2, 4, 8, 256), I32),
        pltpu.VMEM((1024, 16), BF16),
        pltpu.VMEM((2, 16, 2048), BF16),
        pltpu.VMEM((2, 16, 2048), BF16),
        pltpu.VMEM((2, 1024, 1024), BF16),
        pltpu.VMEM((2, 1024, 1024), BF16),
        pltpu.VMEM((2, 256, 256), I32),
        pltpu.VMEM((2, 256, 256), I32),
        pltpu.VMEM((2, 256, 256), I32),
        pltpu.VMEM((2, 8, 32, 256), I32),
        pltpu.VMEM((8, 2, 8, 128), I32),
        pltpu.VMEM((4, 128, 128), I32),
        pltpu.VMEM((4, 1024, 256), BF16),
        pltpu.VMEM((2, 256, 128), I32),
        pltpu.VMEM((2, 256, 128), I32),
        pltpu.VMEM((3, 64, 128), I32),
        pltpu.VMEM((4, 2, 256, 128), I32),
        pltpu.SemaphoreType.REGULAR((5,)),
        dma((16,)), dma((16,)), dma, dma((8,)), dma((8,)), dma, dma, dma((18,)), dma((18,)), dma((16,)), dma((16,)),
        dma((4,)), dma((4,)), dma, dma, dma((3,)), dma((3,)), dma((3,)), dma((3,)), dma((16,)), dma((16,)),
        dma((16,)), dma((16,)), dma((8,)),
    ]
    total = pl.pallas_call(
        kernel,
        out_shape=jax.ShapeDtypeStruct((256, 1024), I32),
        in_specs=[
            pl.BlockSpec(memory_space=pltpu.SMEM),
            pl.BlockSpec(memory_space=pltpu.HBM),
            pl.BlockSpec(memory_space=pltpu.HBM),
        ],
        out_specs=pl.BlockSpec(memory_space=pltpu.HBM),
        scratch_shapes=scratch,
        compiler_params=pltpu.CompilerParams(
            collective_id=0, has_side_effects=True, vmem_limit_bytes=60 * 2**20
        ),
        name="hints",
    )(matrix_seeds, ingest, row_order)
    total = total.reshape(4, 64, 1024)
    low = (total & 65535).astype(F32)
    high = lax.shift_right_logical(total, jnp.int32(16)).astype(F32)
    return jnp.stack([low, high], axis=1) * (1.0 / 65536.0)


def solution(mesh):
    return jax.shard_map(
        on_device, mesh=mesh,
        in_specs=(P(("row", "col"), None), P("row", None), P()),
        out_specs=P(None, None, "col", None), check_vma=False,
    )
```

```python
import functools

import jax
import jax.numpy as jnp
from jax import lax
from jax.experimental import pallas as pl
from jax.experimental.pallas import tpu as pltpu
from jax.sharding import PartitionSpec as P

PRIME = 46337
HALF = 23168
INV = 1.0 / PRIME
MAGIC_ONE = 1.5 * 2.0**23
MAGIC_BYTE = 1.5 * 2.0**31
BIAS = (HALF * 65537 - 0x80808080) % 2**32
BIAS = BIAS - 2**32 if BIAS >= 2**31 else BIAS
NEAR = ((0, 0, 0), (0, 1, 0), (1, 0, 0), (0, 0, 1), (0, 1, 1), (0, 0, -1), (-1, 0, 0), (0, -1, 0))
ORDER = (4, 1, 2, 3, 5, 6, 7, 0)
MESH = pl.DeviceIdType.MESH
F32, BF16, I32 = jnp.float32, jnp.bfloat16, jnp.int32
NT = (((1,), (1,)), ((), ()))
NN = (((1,), (0,)), ((), ()))


def modp(v):
    q = (v.astype(F32) * INV).astype(I32)
    r = v - q * PRIME
    r = jnp.where(r < 0, r + PRIME, r)
    return jnp.where(r >= PRIME, r - PRIME, r)


def centred(v):
    return jnp.where(v > HALF, v - PRIME, v)


def two_digits(v):
    hi = ((v + 128 + 65536) // 256 - 256) * 256
    return hi, v - hi


def pick_rows(rows, shape):
    at = lax.broadcasted_iota(I32, shape, 0)
    out = jnp.zeros(shape, I32)
    for k, row in enumerate(rows):
        out = jnp.where(at == k, row, out)
    return out.astype(F32)


def index_digits(index, seed):
    x = modp(modp(index * 40503) + seed)
    x = modp(x * x)
    hi, lo = two_digits(centred(modp(x * x)))
    nib = [lax.shift_right_logical(x, jnp.int32(4 * k)) & 15 for k in range(4)]
    one = jnp.ones_like(x)
    return pick_rows(nib + nib + [hi, lo, one, one], (16, index.shape[1]))


def column_digits(index):
    b = modp(index * 29989)
    his, los = [], []
    w = modp(b + b)
    for k in range(4):
        hi, lo = two_digits(centred(w))
        his.append(hi)
        los.append(lo)
        w = modp(w * 16)
    hi, lo = two_digits(centred(modp(modp(b * b) + (12345 - HALF + PRIME))))
    one = jnp.ones_like(b)
    return pick_rows(his + los + [one, one, hi, lo], (16, index.shape[1]))


def residue_digits(v):
    q = (v * INV + MAGIC_ONE) - MAGIC_ONE
    r = v - q * PRIME
    hi = (r + MAGIC_BYTE) - MAGIC_BYTE
    return (r - hi).astype(BF16), hi.astype(BF16)


def joined(parts):
    t = parts[0].astype(I32)
    t = t + lax.shift_left((parts[1] * (1.0 / 256)).astype(I32), jnp.int32(8))
    t = t + lax.shift_left(parts[2].astype(I32), jnp.int32(16))
    return t + lax.shift_left((parts[3] * (1.0 / 256)).astype(I32), jnp.int32(24))


def kernel(
    seeds, ingest, order, out,
    rec, order_in, orders, bdig, xdig, xdig2, gen_a, gen_b, give, sib, mine, red, hint_send, hall, a2,
    tot, tsib, zbuf, full, fbuf, known,
    s_in, r_in, s_own, s_ord, r_ord, s_sib, r_sib, s_red, r_red, s_hint, r_hint, s_hx, r_hx, s_tot, r_tot,
    s_z, r_z, s_gz, r_gz, s_gx, r_gx, s_gs, r_gs, s_out,
):
    row, col = lax.axis_index("row"), lax.axis_index("col")
    core, x, zl = row % 2, (row // 2) % 4, row // 8
    y, zh = col % 8, col // 8
    z = zh * 4 + zl

    def dev_at(xx, yy, zz, cc):
        return {"row": ((zz % 4) * 4 + xx) * 2 + cc, "col": (zz // 4) * 8 + yy}

    def dev(dx, dy, dz, other):
        return dev_at((x + dx + 4) % 4, (y + dy + 8) % 8, (z + dz + 8) % 8, (core + other) % 2)

    def dev_line(dz):
        return dev_at(x, y, zh * 4 + (zl + dz) % 4, core)

    def rcopy(src, dst, ssem, rsem, device):
        return pltpu.make_async_remote_copy(
            src_ref=src, dst_ref=dst, send_sem=ssem, recv_sem=rsem, device_id=device, device_id_type=MESH
        )

    sibling = dev(0, 0, 0, 1)

    def arrived(spot, rsem):
        rcopy(spot, spot, s_tot, rsem, sibling).wait_recv()

    order_load = pltpu.make_async_copy(order, order_in, s_own)
    order_load.start()

    barrier = pltpu.get_barrier_semaphore()

    def greet(device, sem):
        pl.semaphore_signal(sem, inc=1, device_id=device, device_id_type=MESH)

    count = 1
    greet(sibling, barrier)
    for off in ((0, 1, 0), (0, -1, 0), (1, 0, 0), (-1, 0, 0), (0, 0, 1), (0, 0, -1), (0, 1, 1), (0, -1, -1)):
        for other in range(2):
            greet(dev(*off, other), barrier)
            count += 1
    pl.semaphore_wait(barrier, count)

    def round_send(k):
        dx, dy, dz = ((1, 0, 0), (0, 1, 0), (0, 2, 0), (0, 0, 1), (0, 0, 2))[k]
        greet(dev(dx, dy, dz, 0), known.at[k])
        greet(dev(-dx, -dy, -dz, 0), known.at[k])

    def round_wait(k):
        pl.semaphore_wait(known.at[k], 2)

    colour = (2 * x + y + 3 * z) % 8
    sign = 1 - 2 * core

    def ingest_src(near, other):
        return ingest.at[:, pl.ds(((colour + near) % 8) * 4096 + ((core + other) % 2) * 2048, 2048)]

    def ingest_copy(near, other):
        slot = near * 2 + core
        device = dev(0, sign, sign, other) if near == 4 else dev(*NEAR[near], other)
        return rcopy(
            ingest_src(near, other), rec.at[pl.ds(slot * 16, 16), :],
            s_in.at[near * 2 + other], r_in.at[slot], device,
        )

    for near in ORDER:
        for other in range(2):
            if near or other:
                ingest_copy(near, other).start()
    own_in = pltpu.make_async_copy(ingest_src(0, 0), rec.at[pl.ds(core * 16, 16), :], r_in.at[core])
    own_in.start()
    round_send(0)

    bdig[...] = jnp.transpose(column_digits(lax.broadcasted_iota(I32, (1, 1024), 1))).astype(BF16)
    index = lax.broadcasted_iota(I32, (1, 2048), 1) + (colour * 4096 + core * 2048)
    for w in range(2):
        xdig[w] = index_digits(index, seeds[0] + 7919 * w).astype(BF16)
    round_wait(0)
    round_send(1)

    def generate(buf, t, kh):
        n_at = pl.multiple_of((((1 - core) * 2 + t) % 4) * 256, 256)
        left = bdig[pl.ds(n_at, 256), :]
        for w in range(2):
            digits = xdig[w, :, kh * 1024 : (kh + 1) * 1024]
            lo, hi = residue_digits(lax.dot_general(left, digits, NN, preferred_element_type=F32))
            buf[(2 * w) * 256 : (2 * w + 1) * 256, :] = lo
            buf[(2 * w + 1) * 256 : (2 * w + 2) * 256, :] = hi

    def multiply(buf, kh):
        r = lax.dot_general(buf[...], rec[:, kh * 1024 : (kh + 1) * 1024], NT, preferred_element_type=F32)
        return joined([r[k * 256 : (k + 1) * 256, :] for k in range(4)])

    for kh in range(2):
        generate(gen_a.at[kh], 0, kh)
    round_wait(1)
    round_send(2)

    for slot in range(16):
        arrived(rec.at[pl.ds(slot * 16, 16), :], r_in.at[slot])
    sums = lax.dot_general(jnp.ones((16, 2048), BF16), rec[...], NT, preferred_element_type=F32)
    bias = sums[0:1, :].astype(I32) * jnp.int32(BIAS)

    gens = (gen_a, gen_b)

    def tile(t):
        acc = bias
        for kh in range(2):
            if t < 3:
                generate(gens[(t + 1) % 2].at[kh], t + 1, kh)
            acc = acc + multiply(gens[t % 2].at[kh], kh)
        return jnp.transpose(acc)

    round_wait(2)
    round_send(3)
    give[0] = tile(0)
    round_wait(3)
    round_send(4)
    give[1] = tile(1)
    round_wait(4)
    sib_copy = rcopy(give, sib, s_sib, r_sib, sibling)
    sib_copy.start()

    order_load.wait()
    orders[0, 0] = jnp.broadcast_to(order_in[...], (8, 256))

    def order_copy(k):
        side, dx = k // 4, k % 4
        zz = 7 - z if side else z
        return rcopy(
            orders.at[0, 0], orders.at[side, dx], s_ord.at[k], r_ord.at[k], dev_at((x + dx) % 4, y, zz, core)
        )

    for k in range(1, 8):
        order_copy(k).start()

    def red_copy(q, near):
        if near in (4, 8):
            at, sg = (near // 4 - 1) * 16, 1 if near == 8 else -1
            rows, dst, device = 128 + at, red.at[q, 4, pl.ds(at, 16), :], dev(0, sg, sg, 0)
            rows = mine.at[q, pl.ds(rows, 16), :]
        else:
            dx, dy, dz = NEAR[near]
            rows, dst, device = mine.at[q, pl.ds(near * 32, 32), :], red.at[q, near], dev(-dx, -dy, -dz, 0)
        return rcopy(rows, dst, s_red.at[q * 9 + near], r_red.at[q * 9 + near], device)

    for q in range(2):
        acc = tile(2 + q)
        if q == 0:
            sib_copy.wait_recv()
        mine[q] = acc + sib[q]
        for near in (4, 8, 1, 2, 3, 5, 6, 7):
            red_copy(q, near).start()
    lane = lax.broadcasted_iota(I32, (1, 2048), 1)
    mirrored = (lane // 256) % 2
    block = ((zl + mirrored * (3 - 2 * zl)) * 4 + (x + 4 - lane // 512) % 4) * 2 + core
    for w in range(2):
        xdig2[w] = index_digits(block * 256 + lane % 256, seeds[1] + 7919 * w).astype(BF16)

    for k in range(1, 8):
        arrived(orders.at[k // 4, k % 4], r_ord.at[k])
    spot = lax.broadcasted_iota(I32, (256, 1), 0)
    side = (spot // 64) % 2
    ingest_row = ((zh + side * (1 - 2 * zh)) * 8 + (spot // 8) % 8) * 16 + (spot // 128) * 8 + spot % 8
    wanted = ingest_row + 256 * side
    lane = lax.broadcasted_iota(I32, (1, 512), 1)
    quarter = bdig[pl.ds(pl.multiple_of(x * 256, 256), 256), :]

    def second_rows(dx):
        have = jnp.concatenate([orders[0, dx, 0:1, :], orders[1, dx, 0:1, :]], axis=1) + (lane // 256) * 256
        onehot = (wanted == have).astype(F32).astype(BF16)
        for w in range(2):
            digits = xdig2[w, :, dx * 512 : (dx + 1) * 512]
            perm = lax.dot_general(onehot, digits, NT, preferred_element_type=F32).astype(BF16)
            lo, hi = residue_digits(lax.dot_general(perm, quarter, NT, preferred_element_type=F32))
            a2[2 * w, dx * 256 : (dx + 1) * 256, :] = lo
            a2[2 * w + 1, dx * 256 : (dx + 1) * 256, :] = hi

    second_rows(0)
    second_rows(1)
    hints = []
    for q in range(2):
        hint = mine[q, 0:32, :]
        for near in (1, 2, 3, 5, 6, 7, 4, 8):
            red_copy(q, near).wait_recv()
        for near in range(1, 8):
            hint = hint + red[q, near]
        hints.append(hint)

    low_lane = lax.broadcasted_iota(I32, (8, 128), 1) < 64
    for t in range(4):
        for cc in range(2):
            tile_at = hints[t // 2][cc * 16 : (cc + 1) * 16, (t % 2) * 128 : (t % 2 + 1) * 128]
            top, low = tile_at[0:8, :], tile_at[8:16, :]
            hint_send[2 * t, cc] = jnp.where(low_lane, top, pltpu.roll(low, 64, 1))
            hint_send[2 * t + 1, cc] = jnp.where(low_lane, pltpu.roll(top, 64, 1), low)
    away = (zh + core) % 2
    local = away == 0
    landing = hall.at[0, pl.ds((away * 8 + y) * 8, 8), :]
    landed = r_hint.at[away * 8 + y]

    def hint_copy(dy, other):
        yy = (y + dy) % 8
        return rcopy(
            hint_send.at[yy, (core + other) % 2], landing, s_hint.at[dy * 2 + other], landed,
            dev_at(x, yy, z + away * (7 - 2 * z), (core + other) % 2),
        )

    own_hint = pltpu.make_async_copy(hint_send.at[y, core], landing, landed)
    for dy in (4, 3, 5, 2, 6, 1, 7, 0):
        for other in range(2):
            if dy or other:
                hint_copy(dy, other).start()
            else:
                @pl.when(local)
                def _():
                    own_hint.start()

                @pl.when(jnp.logical_not(local))
                def _():
                    hint_copy(0, 0).start()

    second_rows(3)
    second_rows(2)
    for k in range(16):
        arrived(hall.at[0, pl.ds(k * 8, 8), :], r_hint.at[k])

    def hx_copy(k):
        if k < 2:
            return rcopy(hall.at[0], hall.at[1 + 2 * k], s_hx.at[k], r_hx.at[k], dev(1 - 2 * k, 0, 0, 0))
        at = pl.ds((k - 2) * 64, 64)
        return rcopy(
            hall.at[2 * k - 3, at, :], hall.at[2, at, :], s_hx.at[k], r_hx.at[k], dev(5 - 2 * k, 0, 0, 0)
        )

    for k in range(2):
        hx_copy(k).start()

    def second(dx, total):
        turned = jnp.transpose(hall[dx])
        wide = jnp.concatenate([turned[0:64, :], turned[64:128, :]], axis=1)
        left = jnp.concatenate(
            [
                ((lax.shift_right_logical(wide, jnp.int32(8 * d)) & 255) - 128).astype(F32).astype(BF16)
                for d in range(4)
            ],
            axis=0,
        )
        lsum = lax.dot_general(left, jnp.ones((256, 128), BF16), NN, preferred_element_type=F32)
        term = joined(
            [
                lax.dot_general(left, a2[k, dx * 256 : (dx + 1) * 256, :], NN, preferred_element_type=F32)
                for k in range(4)
            ]
        )
        term = term + lsum[:, 0:1].astype(I32) * jnp.int32(BIAS)
        return term if total is None else total + term

    total = second(0, None)
    hx_copy(0).wait_recv()
    hx_copy(2).start()
    hx_copy(1).wait_recv()
    hx_copy(3).start()
    total = second(1, total)
    total = second(3, total)
    hx_copy(2).wait_recv()
    hx_copy(3).wait_recv()
    total = second(2, total)
    tot[0] = total[:, 0:128]
    tot[1] = total[:, 128:256]

    tot_copy = rcopy(tot.at[1 - core], tsib.at[0], s_tot, r_tot, sibling)
    tot_copy.start()
    tot_copy.wait_recv()
    tsib[1] = tot[core] + tsib[0]

    def z_copy(dz):
        zz = (zl + dz) % 4
        return rcopy(
            tsib.at[1, pl.ds(zz * 64, 64), :], zbuf.at[dz - 1], s_z.at[dz - 1], r_z.at[dz - 1], dev_line(dz)
        )

    for dz in (1, 3, 2):
        z_copy(dz).start()
    acc = tsib[1, pl.ds(pl.multiple_of(zl * 64, 64), 64), :]
    for dz in (1, 3, 2):
        z_copy(dz).wait_recv()
        acc = acc + zbuf[dz - 1]
    full[x, core, pl.ds(pl.multiple_of(zl * 64, 64), 64), :] = acc

    def part_of(dx, j, cc):
        return full.at[(x + 4 - dx) % 4, cc, pl.ds(((zl + 4 - j) % 4) * 64, 64), :]

    def half_of(dx, j, k):
        return full.at[(x + 4 - dx) % 4, core, pl.ds(((zl + 4 - j) % 4) * 64 + k * 32, 32), :]

    def gz_copy(dz):
        return rcopy(part_of(0, 0, core), part_of(0, 0, core), s_gz.at[dz - 1], r_gz.at[dz - 1], dev_line(dz))

    def gx_copy(j, k):
        spot = part_of(0, j, core) if k < 2 else half_of(2 * k - 3, j, k - 2)
        step = 1 - 2 * (k % 2)
        return rcopy(spot, spot, s_gx.at[j * 4 + k], r_gx.at[j * 4 + k], dev(step, 0, 0, 0))

    def out_at(dx, j, cc):
        return out.at[(zl + 4 - j) % 4, :, :, pl.ds(((x + 4 - dx) % 4) * 256 + cc * 128, 128)]

    def gs_copy(dx, j):
        k = dx * 4 + j
        return rcopy(fbuf.at[dx, j], out_at(dx, j, core), s_gs.at[k], r_gs.at[k], sibling)

    def out_copy(dx, j):
        return pltpu.make_async_copy(fbuf.at[dx, j], out_at(dx, j, core), s_out.at[dx * 4 + j])

    def emit(dx, j):
        value = full[(x + 4 - dx) % 4, core, pl.ds(pl.multiple_of(((zl + 4 - j) % 4) * 64, 64), 64), :]
        fbuf[dx, j, 0] = (value & 65535).astype(F32) * (1.0 / 65536.0)
        fbuf[dx, j, 1] = lax.shift_right_logical(value, jnp.int32(16)).astype(F32) * (1.0 / 65536.0)
        gs_copy(dx, j).start()
        out_copy(dx, j).start()

    def spread(j):
        gx_copy(j, 0).start()
        gx_copy(j, 1).start()
        emit(0, j)

    def forward(j):
        arrived(part_of(1, j, core), r_gx.at[j * 4])
        gx_copy(j, 2).start()
        arrived(part_of(3, j, core), r_gx.at[j * 4 + 1])
        gx_copy(j, 3).start()
        emit(1, j)
        emit(3, j)

    def finish(j):
        arrived(half_of(2, j, 0), r_gx.at[j * 4 + 2])
        arrived(half_of(2, j, 1), r_gx.at[j * 4 + 3])
        emit(2, j)

    for dz in (2, 1, 3):
        gz_copy(dz).start()
    spread(0)
    arrived(part_of(0, 1, core), r_gz.at[0])
    spread(1)
    arrived(part_of(0, 3, core), r_gz.at[2])
    spread(3)
    forward(0)
    arrived(part_of(0, 2, core), r_gz.at[1])
    spread(2)
    for j in (1, 3, 2):
        forward(j)
    for j in (0, 1, 3, 2):
        finish(j)
    for dx in (0, 1, 3, 2):
        for j in (0, 1, 3, 2):
            arrived(out_at(dx, j, 1 - core), r_gs.at[dx * 4 + j])

    for near in range(8):
        for other in range(2):
            if near or other:
                ingest_copy(near, other).wait_send()
    for k in range(1, 8):
        order_copy(k).wait_send()
    sib_copy.wait_send()
    for q in range(2):
        for near in range(1, 9):
            red_copy(q, near).wait_send()
    for dy in range(8):
        for other in range(2):
            if dy or other:
                hint_copy(dy, other).wait_send()
            else:
                @pl.when(jnp.logical_not(local))
                def _():
                    hint_copy(0, 0).wait_send()
    for k in range(4):
        hx_copy(k).wait_send()
    tot_copy.wait_send()
    for d in range(1, 4):
        z_copy(d).wait_send()
        gz_copy(d).wait_send()
    for j in range(4):
        for k in range(4):
            gx_copy(j, k).wait_send()
            gs_copy(k, j).wait_send()
    for dx in range(4):
        for j in range(4):
            out_copy(dx, j).wait()


def on_device(ingest, row_order, matrix_seeds):
    dma = pltpu.SemaphoreType.DMA
    scratch = [
        pltpu.VMEM((256, 2048), BF16),
        pltpu.VMEM((1, 256), I32),
        pltpu.VMEM((2, 4, 8, 256), I32),
        pltpu.VMEM((1024, 16), BF16),
        pltpu.VMEM((2, 16, 2048), BF16),
        pltpu.VMEM((2, 16, 2048), BF16),
        pltpu.VMEM((2, 1024, 1024), BF16),
        pltpu.VMEM((2, 1024, 1024), BF16),
        pltpu.VMEM((2, 256, 256), I32),
        pltpu.VMEM((2, 256, 256), I32),
        pltpu.VMEM((2, 256, 256), I32),
        pltpu.VMEM((2, 8, 32, 256), I32),
        pltpu.VMEM((8, 2, 8, 128), I32),
        pltpu.VMEM((4, 128, 128), I32),
        pltpu.VMEM((4, 1024, 256), BF16),
        pltpu.VMEM((2, 256, 128), I32),
        pltpu.VMEM((2, 256, 128), I32),
        pltpu.VMEM((3, 64, 128), I32),
        pltpu.VMEM((4, 2, 256, 128), I32),
        pltpu.VMEM((4, 4, 2, 64, 128), F32),
        pltpu.SemaphoreType.REGULAR((5,)),
        dma((16,)), dma((16,)), dma, dma((8,)), dma((8,)), dma, dma, dma((18,)), dma((18,)), dma((16,)), dma((16,)),
        dma((4,)), dma((4,)), dma, dma, dma((3,)), dma((3,)), dma((3,)), dma((3,)), dma((16,)), dma((16,)),
        dma((16,)), dma((16,)), dma((16,)),
    ]
    return pl.pallas_call(
        kernel,
        out_shape=jax.ShapeDtypeStruct((4, 2, 64, 1024), F32),
        in_specs=[
            pl.BlockSpec(memory_space=pltpu.SMEM),
            pl.BlockSpec(memory_space=pltpu.HBM),
            pl.BlockSpec(memory_space=pltpu.HBM),
        ],
        out_specs=pl.BlockSpec(memory_space=pltpu.HBM),
        scratch_shapes=scratch,
        compiler_params=pltpu.CompilerParams(
            collective_id=0, has_side_effects=True, vmem_limit_bytes=60 * 2**20
        ),
        name="hints",
    )(matrix_seeds, ingest, row_order)


def solution(mesh):
    return jax.shard_map(
        on_device, mesh=mesh,
        in_specs=(P(("row", "col"), None), P("row", None), P()),
        out_specs=P(None, None, "col", None), check_vma=False,
    )
```

```python
import functools

import jax
import jax.numpy as jnp
from jax import lax
from jax.experimental import pallas as pl
from jax.experimental.pallas import tpu as pltpu
from jax.sharding import PartitionSpec as P

PRIME = 46337
HALF = 23168
INV = 1.0 / PRIME
MAGIC_ONE = 1.5 * 2.0**23
MAGIC_BYTE = 1.5 * 2.0**31
BIAS = (HALF * 65537 - 0x80808080) % 2**32
BIAS = BIAS - 2**32 if BIAS >= 2**31 else BIAS
NEAR = ((0, 0, 0), (0, 1, 0), (1, 0, 0), (0, 0, 1), (0, 1, 1), (0, 0, -1), (-1, 0, 0), (0, -1, 0))
ORDER = (4, 1, 2, 3, 5, 6, 7, 0)
MESH = pl.DeviceIdType.MESH
F32, BF16, I32 = jnp.float32, jnp.bfloat16, jnp.int32
NT = (((1,), (1,)), ((), ()))
NN = (((1,), (0,)), ((), ()))


def modp(v):
    q = (v.astype(F32) * INV).astype(I32)
    r = v - q * PRIME
    r = jnp.where(r < 0, r + PRIME, r)
    return jnp.where(r >= PRIME, r - PRIME, r)


def centred(v):
    return jnp.where(v > HALF, v - PRIME, v)


def two_digits(v):
    hi = ((v + 128 + 65536) // 256 - 256) * 256
    return hi, v - hi


def pick_rows(rows, shape):
    at = lax.broadcasted_iota(I32, shape, 0)
    out = jnp.zeros(shape, I32)
    for k, row in enumerate(rows):
        out = jnp.where(at == k, row, out)
    return out.astype(F32)


def index_digits(index, seed):
    x = modp(modp(index * 40503) + seed)
    x = modp(x * x)
    hi, lo = two_digits(centred(modp(x * x)))
    nib = [lax.shift_right_logical(x, jnp.int32(4 * k)) & 15 for k in range(4)]
    one = jnp.ones_like(x)
    return pick_rows(nib + nib + [hi, lo, one, one], (16, index.shape[1]))


def column_digits(index):
    b = modp(index * 29989)
    his, los = [], []
    w = modp(b + b)
    for k in range(4):
        hi, lo = two_digits(centred(w))
        his.append(hi)
        los.append(lo)
        w = modp(w * 16)
    hi, lo = two_digits(centred(modp(modp(b * b) + (12345 - HALF + PRIME))))
    one = jnp.ones_like(b)
    return pick_rows(his + los + [one, one, hi, lo], (16, index.shape[1]))


def residue_digits(v):
    q = (v * INV + MAGIC_ONE) - MAGIC_ONE
    r = v - q * PRIME
    hi = (r + MAGIC_BYTE) - MAGIC_BYTE
    return (r - hi).astype(BF16), hi.astype(BF16)


def joined(parts):
    t = parts[0].astype(I32)
    t = t + lax.shift_left((parts[1] * (1.0 / 256)).astype(I32), jnp.int32(8))
    t = t + lax.shift_left(parts[2].astype(I32), jnp.int32(16))
    return t + lax.shift_left((parts[3] * (1.0 / 256)).astype(I32), jnp.int32(24))


def kernel(
    seeds, ingest, order, out,
    rec, order_in, orders, bdig, xdig, xdig2, gen_a, gen_b, give, sib, mine, red, hint_send, hall, a2,
    tot, tsib, zbuf, full, known,
    s_in, r_in, s_own, s_ord, r_ord, s_sib, r_sib, s_red, r_red, s_hint, r_hint, s_hx, r_hx, s_tot, r_tot,
    s_z, r_z, s_gz, r_gz, s_gx, r_gx, s_gs, r_gs, s_out,
):
    row, col = lax.axis_index("row"), lax.axis_index("col")
    core, x, zl = row % 2, (row // 2) % 4, row // 8
    y, zh = col % 8, col // 8
    z = zh * 4 + zl

    def dev_at(xx, yy, zz, cc):
        return {"row": ((zz % 4) * 4 + xx) * 2 + cc, "col": (zz // 4) * 8 + yy}

    def dev(dx, dy, dz, other):
        return dev_at((x + dx + 4) % 4, (y + dy + 8) % 8, (z + dz + 8) % 8, (core + other) % 2)

    def dev_line(dz):
        return dev_at(x, y, zh * 4 + (zl + dz) % 4, core)

    def rcopy(src, dst, ssem, rsem, device):
        return pltpu.make_async_remote_copy(
            src_ref=src, dst_ref=dst, send_sem=ssem, recv_sem=rsem, device_id=device, device_id_type=MESH
        )

    sibling = dev(0, 0, 0, 1)

    def arrived(spot, rsem):
        rcopy(spot, spot, s_tot, rsem, sibling).wait_recv()

    order_load = pltpu.make_async_copy(order, order_in, s_own)
    order_load.start()

    barrier = pltpu.get_barrier_semaphore()

    def greet(device, sem):
        pl.semaphore_signal(sem, inc=1, device_id=device, device_id_type=MESH)

    count = 1
    greet(sibling, barrier)
    for off in ((0, 1, 0), (0, -1, 0), (1, 0, 0), (-1, 0, 0), (0, 0, 1), (0, 0, -1), (0, 1, 1), (0, -1, -1)):
        for other in range(2):
            greet(dev(*off, other), barrier)
            count += 1
    pl.semaphore_wait(barrier, count)

    def round_send(k):
        dx, dy, dz = ((1, 0, 0), (0, 1, 0), (0, 2, 0), (0, 0, 1), (0, 0, 2))[k]
        greet(dev(dx, dy, dz, 0), known.at[k])
        greet(dev(-dx, -dy, -dz, 0), known.at[k])

    def round_wait(k):
        pl.semaphore_wait(known.at[k], 2)

    colour = (2 * x + y + 3 * z) % 8
    sign = 1 - 2 * core

    def ingest_src(near, other):
        return ingest.at[:, pl.ds(((colour + near) % 8) * 4096 + ((core + other) % 2) * 2048, 2048)]

    def ingest_copy(near, other):
        slot = near * 2 + core
        device = dev(0, sign, sign, other) if near == 4 else dev(*NEAR[near], other)
        return rcopy(
            ingest_src(near, other), rec.at[pl.ds(slot * 16, 16), :],
            s_in.at[near * 2 + other], r_in.at[slot], device,
        )

    for near in ORDER:
        for other in range(2):
            if near or other:
                ingest_copy(near, other).start()
    own_in = pltpu.make_async_copy(ingest_src(0, 0), rec.at[pl.ds(core * 16, 16), :], r_in.at[core])
    own_in.start()
    round_send(0)

    bdig[...] = jnp.transpose(column_digits(lax.broadcasted_iota(I32, (1, 1024), 1))).astype(BF16)
    index = lax.broadcasted_iota(I32, (1, 2048), 1) + (colour * 4096 + core * 2048)
    for w in range(2):
        xdig[w] = index_digits(index, seeds[0] + 7919 * w).astype(BF16)
    round_wait(0)
    round_send(1)

    def generate(buf, t, kh):
        n_at = pl.multiple_of((((1 - core) * 2 + t) % 4) * 256, 256)
        left = bdig[pl.ds(n_at, 256), :]
        for w in range(2):
            digits = xdig[w, :, kh * 1024 : (kh + 1) * 1024]
            lo, hi = residue_digits(lax.dot_general(left, digits, NN, preferred_element_type=F32))
            buf[(2 * w) * 256 : (2 * w + 1) * 256, :] = lo
            buf[(2 * w + 1) * 256 : (2 * w + 2) * 256, :] = hi

    def multiply(buf, kh):
        r = lax.dot_general(buf[...], rec[:, kh * 1024 : (kh + 1) * 1024], NT, preferred_element_type=F32)
        return joined([r[k * 256 : (k + 1) * 256, :] for k in range(4)])

    for kh in range(2):
        generate(gen_a.at[kh], 0, kh)
    round_wait(1)
    round_send(2)

    for slot in range(16):
        arrived(rec.at[pl.ds(slot * 16, 16), :], r_in.at[slot])
    sums = lax.dot_general(jnp.ones((16, 2048), BF16), rec[...], NT, preferred_element_type=F32)
    bias = sums[0:1, :].astype(I32) * jnp.int32(BIAS)

    gens = (gen_a, gen_b)

    def tile(t):
        acc = bias
        for kh in range(2):
            if t < 3:
                generate(gens[(t + 1) % 2].at[kh], t + 1, kh)
            acc = acc + multiply(gens[t % 2].at[kh], kh)
        return jnp.transpose(acc)

    round_wait(2)
    round_send(3)
    give[0] = tile(0)
    round_wait(3)
    round_send(4)
    give[1] = tile(1)
    round_wait(4)
    sib_copy = rcopy(give, sib, s_sib, r_sib, sibling)
    sib_copy.start()

    order_load.wait()
    orders[0, 0] = jnp.broadcast_to(order_in[...], (8, 256))

    def order_copy(k):
        side, dx = k // 4, k % 4
        zz = 7 - z if side else z
        return rcopy(
            orders.at[0, 0], orders.at[side, dx], s_ord.at[k], r_ord.at[k], dev_at((x + dx) % 4, y, zz, core)
        )

    for k in range(1, 8):
        order_copy(k).start()

    def red_copy(q, near):
        if near in (4, 8):
            at, sg = (near // 4 - 1) * 16, 1 if near == 8 else -1
            rows, dst, device = 128 + at, red.at[q, 4, pl.ds(at, 16), :], dev(0, sg, sg, 0)
            rows = mine.at[q, pl.ds(rows, 16), :]
        else:
            dx, dy, dz = NEAR[near]
            rows, dst, device = mine.at[q, pl.ds(near * 32, 32), :], red.at[q, near], dev(-dx, -dy, -dz, 0)
        return rcopy(rows, dst, s_red.at[q * 9 + near], r_red.at[q * 9 + near], device)

    for q in range(2):
        acc = tile(2 + q)
        if q == 0:
            sib_copy.wait_recv()
        mine[q] = acc + sib[q]
        for near in (4, 8, 1, 2, 3, 5, 6, 7):
            red_copy(q, near).start()
    lane = lax.broadcasted_iota(I32, (1, 2048), 1)
    mirrored = (lane // 256) % 2
    block = ((zl + mirrored * (3 - 2 * zl)) * 4 + (x + 4 - lane // 512) % 4) * 2 + core
    for w in range(2):
        xdig2[w] = index_digits(block * 256 + lane % 256, seeds[1] + 7919 * w).astype(BF16)

    for k in range(1, 8):
        arrived(orders.at[k // 4, k % 4], r_ord.at[k])
    spot = lax.broadcasted_iota(I32, (256, 1), 0)
    side = (spot // 64) % 2
    ingest_row = ((zh + side * (1 - 2 * zh)) * 8 + (spot // 8) % 8) * 16 + (spot // 128) * 8 + spot % 8
    wanted = ingest_row + 256 * side
    lane = lax.broadcasted_iota(I32, (1, 512), 1)
    quarter = bdig[pl.ds(pl.multiple_of(x * 256, 256), 256), :]

    def second_rows(dx):
        have = jnp.concatenate([orders[0, dx, 0:1, :], orders[1, dx, 0:1, :]], axis=1) + (lane // 256) * 256
        onehot = (wanted == have).astype(F32).astype(BF16)
        for w in range(2):
            digits = xdig2[w, :, dx * 512 : (dx + 1) * 512]
            perm = lax.dot_general(onehot, digits, NT, preferred_element_type=F32).astype(BF16)
            lo, hi = residue_digits(lax.dot_general(perm, quarter, NT, preferred_element_type=F32))
            a2[2 * w, dx * 256 : (dx + 1) * 256, :] = lo
            a2[2 * w + 1, dx * 256 : (dx + 1) * 256, :] = hi

    second_rows(0)
    second_rows(1)
    hints = []
    for q in range(2):
        hint = mine[q, 0:32, :]
        for near in (1, 2, 3, 5, 6, 7, 4, 8):
            red_copy(q, near).wait_recv()
        for near in range(1, 8):
            hint = hint + red[q, near]
        hints.append(hint)

    low_lane = lax.broadcasted_iota(I32, (8, 128), 1) < 64
    for t in range(4):
        for cc in range(2):
            tile_at = hints[t // 2][cc * 16 : (cc + 1) * 16, (t % 2) * 128 : (t % 2 + 1) * 128]
            top, low = tile_at[0:8, :], tile_at[8:16, :]
            hint_send[2 * t, cc] = jnp.where(low_lane, top, pltpu.roll(low, 64, 1))
            hint_send[2 * t + 1, cc] = jnp.where(low_lane, pltpu.roll(top, 64, 1), low)
    away = (zh + core) % 2
    local = away == 0
    landing = hall.at[0, pl.ds((away * 8 + y) * 8, 8), :]
    landed = r_hint.at[away * 8 + y]

    def hint_copy(dy, other):
        yy = (y + dy) % 8
        return rcopy(
            hint_send.at[yy, (core + other) % 2], landing, s_hint.at[dy * 2 + other], landed,
            dev_at(x, yy, z + away * (7 - 2 * z), (core + other) % 2),
        )

    own_hint = pltpu.make_async_copy(hint_send.at[y, core], landing, landed)
    for dy in (4, 3, 5, 2, 6, 1, 7, 0):
        for other in range(2):
            if dy or other:
                hint_copy(dy, other).start()
            else:
                @pl.when(local)
                def _():
                    own_hint.start()

                @pl.when(jnp.logical_not(local))
                def _():
                    hint_copy(0, 0).start()

    second_rows(3)
    second_rows(2)
    for k in range(16):
        arrived(hall.at[0, pl.ds(k * 8, 8), :], r_hint.at[k])

    def hx_copy(k):
        if k < 2:
            return rcopy(hall.at[0], hall.at[1 + 2 * k], s_hx.at[k], r_hx.at[k], dev(1 - 2 * k, 0, 0, 0))
        at = pl.ds((k - 2) * 64, 64)
        return rcopy(
            hall.at[2 * k - 3, at, :], hall.at[2, at, :], s_hx.at[k], r_hx.at[k], dev(5 - 2 * k, 0, 0, 0)
        )

    for k in range(2):
        hx_copy(k).start()

    def second(dx, total):
        turned = jnp.transpose(hall[dx])
        wide = jnp.concatenate([turned[0:64, :], turned[64:128, :]], axis=1)
        left = jnp.concatenate(
            [
                ((lax.shift_right_logical(wide, jnp.int32(8 * d)) & 255) - 128).astype(F32).astype(BF16)
                for d in range(4)
            ],
            axis=0,
        )
        lsum = lax.dot_general(left, jnp.ones((256, 128), BF16), NN, preferred_element_type=F32)
        term = joined(
            [
                lax.dot_general(left, a2[k, dx * 256 : (dx + 1) * 256, :], NN, preferred_element_type=F32)
                for k in range(4)
            ]
        )
        term = term + lsum[:, 0:1].astype(I32) * jnp.int32(BIAS)
        return term if total is None else total + term

    total = second(0, None)
    hx_copy(0).wait_recv()
    hx_copy(2).start()
    hx_copy(1).wait_recv()
    hx_copy(3).start()
    total = second(1, total)
    total = second(3, total)
    hx_copy(2).wait_recv()
    hx_copy(3).wait_recv()
    total = second(2, total)
    tot[0] = total[:, 0:128]
    tot[1] = total[:, 128:256]

    tot_copy = rcopy(tot.at[1 - core], tsib.at[0], s_tot, r_tot, sibling)
    tot_copy.start()
    tot_copy.wait_recv()
    tsib[1] = tot[core] + tsib[0]

    def z_copy(dz):
        zz = (zl + dz) % 4
        return rcopy(
            tsib.at[1, pl.ds(zz * 64, 64), :], zbuf.at[dz - 1], s_z.at[dz - 1], r_z.at[dz - 1], dev_line(dz)
        )

    for dz in (1, 3, 2):
        z_copy(dz).start()
    acc = tsib[1, pl.ds(pl.multiple_of(zl * 64, 64), 64), :]
    for dz in (1, 3, 2):
        z_copy(dz).wait_recv()
        acc = acc + zbuf[dz - 1]
    full[x, core, pl.ds(pl.multiple_of(zl * 64, 64), 64), :] = acc

    def part_of(dx, j, cc):
        return full.at[(x + 4 - dx) % 4, cc, pl.ds(((zl + 4 - j) % 4) * 64, 64), :]

    def half_of(dx, j, k):
        return full.at[(x + 4 - dx) % 4, core, pl.ds(((zl + 4 - j) % 4) * 64 + k * 32, 32), :]

    def gz_copy(dz):
        return rcopy(part_of(0, 0, core), part_of(0, 0, core), s_gz.at[dz - 1], r_gz.at[dz - 1], dev_line(dz))

    def gx_copy(j, k):
        spot = part_of(0, j, core) if k < 2 else half_of(2 * k - 3, j, k - 2)
        step = 1 - 2 * (k % 2)
        return rcopy(spot, spot, s_gx.at[j * 4 + k], r_gx.at[j * 4 + k], dev(step, 0, 0, 0))

    def out_at(dx, j, cc):
        return out.at[pl.ds(((zl + 4 - j) % 4) * 64, 64), pl.ds(((x + 4 - dx) % 4) * 256 + cc * 128, 128)]

    def gs_copy(dx, j):
        k = dx * 4 + j
        return rcopy(part_of(dx, j, core), out_at(dx, j, core), s_gs.at[k], r_gs.at[k], sibling)

    def out_copy(dx, j):
        return pltpu.make_async_copy(part_of(dx, j, core), out_at(dx, j, core), s_out.at[dx * 4 + j])

    def emit(dx, j):
        gs_copy(dx, j).start()
        out_copy(dx, j).start()

    def spread(j):
        gx_copy(j, 0).start()
        gx_copy(j, 1).start()
        emit(0, j)

    def forward(j):
        arrived(part_of(1, j, core), r_gx.at[j * 4])
        gx_copy(j, 2).start()
        arrived(part_of(3, j, core), r_gx.at[j * 4 + 1])
        gx_copy(j, 3).start()
        emit(1, j)
        emit(3, j)

    def finish(j):
        arrived(half_of(2, j, 0), r_gx.at[j * 4 + 2])
        arrived(half_of(2, j, 1), r_gx.at[j * 4 + 3])
        emit(2, j)

    close = 3 - 2 * (zl // 2)
    chunks = (0, close, 2, 4 - close)
    for dz in (2, 1, 3):
        gz_copy(dz).start()
    spread(0)
    for k in range(1, 4):
        arrived(part_of(0, chunks[k], core), r_gz.at[chunks[k] - 1])
        spread(chunks[k])
        forward(chunks[k - 1])
    forward(chunks[3])
    for j in chunks:
        finish(j)
    for dx in range(4):
        for j in range(4):
            arrived(out_at(dx, j, 1 - core), r_gs.at[dx * 4 + j])

    for near in range(8):
        for other in range(2):
            if near or other:
                ingest_copy(near, other).wait_send()
    for k in range(1, 8):
        order_copy(k).wait_send()
    sib_copy.wait_send()
    for q in range(2):
        for near in range(1, 9):
            red_copy(q, near).wait_send()
    for dy in range(8):
        for other in range(2):
            if dy or other:
                hint_copy(dy, other).wait_send()
            else:
                @pl.when(jnp.logical_not(local))
                def _():
                    hint_copy(0, 0).wait_send()
    for k in range(4):
        hx_copy(k).wait_send()
    tot_copy.wait_send()
    for d in range(1, 4):
        z_copy(d).wait_send()
        gz_copy(d).wait_send()
    for j in range(4):
        for k in range(4):
            gx_copy(j, k).wait_send()
            gs_copy(k, j).wait_send()
    for dx in range(4):
        for j in range(4):
            out_copy(dx, j).wait()


def halves(total, out):
    value = total[...]
    out[0, 0] = (value & 65535).astype(F32) * (1.0 / 65536.0)
    out[0, 1] = lax.shift_right_logical(value, jnp.int32(16)).astype(F32) * (1.0 / 65536.0)


def on_device(ingest, row_order, matrix_seeds):
    dma = pltpu.SemaphoreType.DMA
    scratch = [
        pltpu.VMEM((256, 2048), BF16),
        pltpu.VMEM((1, 256), I32),
        pltpu.VMEM((2, 4, 8, 256), I32),
        pltpu.VMEM((1024, 16), BF16),
        pltpu.VMEM((2, 16, 2048), BF16),
        pltpu.VMEM((2, 16, 2048), BF16),
        pltpu.VMEM((2, 1024, 1024), BF16),
        pltpu.VMEM((2, 1024, 1024), BF16),
        pltpu.VMEM((2, 256, 256), I32),
        pltpu.VMEM((2, 256, 256), I32),
        pltpu.VMEM((2, 256, 256), I32),
        pltpu.VMEM((2, 8, 32, 256), I32),
        pltpu.VMEM((8, 2, 8, 128), I32),
        pltpu.VMEM((4, 128, 128), I32),
        pltpu.VMEM((4, 1024, 256), BF16),
        pltpu.VMEM((2, 256, 128), I32),
        pltpu.VMEM((2, 256, 128), I32),
        pltpu.VMEM((3, 64, 128), I32),
        pltpu.VMEM((4, 2, 256, 128), I32),
        pltpu.SemaphoreType.REGULAR((5,)),
        dma((16,)), dma((16,)), dma, dma((8,)), dma((8,)), dma, dma, dma((18,)), dma((18,)), dma((16,)), dma((16,)),
        dma((4,)), dma((4,)), dma, dma, dma((3,)), dma((3,)), dma((3,)), dma((3,)), dma((16,)), dma((16,)),
        dma((16,)), dma((16,)), dma((16,)),
    ]
    total = pl.pallas_call(
        kernel,
        out_shape=jax.ShapeDtypeStruct((256, 1024), I32),
        in_specs=[
            pl.BlockSpec(memory_space=pltpu.SMEM),
            pl.BlockSpec(memory_space=pltpu.HBM),
            pl.BlockSpec(memory_space=pltpu.HBM),
        ],
        out_specs=pl.BlockSpec(memory_space=pltpu.HBM),
        scratch_shapes=scratch,
        compiler_params=pltpu.CompilerParams(
            collective_id=0, has_side_effects=True, vmem_limit_bytes=60 * 2**20
        ),
        name="hints",
    )(matrix_seeds, ingest, row_order)
    return pl.pallas_call(
        halves,
        grid=(4,),
        out_shape=jax.ShapeDtypeStruct((4, 2, 64, 1024), F32),
        in_specs=[pl.BlockSpec((64, 1024), lambda d: (d, 0))],
        out_specs=pl.BlockSpec((1, 2, 64, 1024), lambda d: (d, 0, 0, 0)),
        name="halves",
    )(total)


def solution(mesh):
    return jax.shard_map(
        on_device, mesh=mesh,
        in_specs=(P(("row", "col"), None), P("row", None), P()),
        out_specs=P(None, None, "col", None), check_vma=False,
    )
```

```python
import functools

import jax
import jax.numpy as jnp
from jax import lax
from jax.experimental import pallas as pl
from jax.experimental.pallas import tpu as pltpu
from jax.sharding import PartitionSpec as P

PRIME = 46337
HALF = 23168
INV = 1.0 / PRIME
MAGIC_ONE = 1.5 * 2.0**23
MAGIC_BYTE = 1.5 * 2.0**31
BIAS = (HALF * 65537 - 0x80808080) % 2**32
BIAS = BIAS - 2**32 if BIAS >= 2**31 else BIAS
NEAR = ((0, 0, 0), (0, 1, 0), (1, 0, 0), (0, 0, 1), (0, 1, 1), (0, 0, -1), (-1, 0, 0), (0, -1, 0))
ORDER = (4, 1, 2, 3, 5, 6, 7, 0)
MESH = pl.DeviceIdType.MESH
F32, BF16, I32 = jnp.float32, jnp.bfloat16, jnp.int32
NT = (((1,), (1,)), ((), ()))
NN = (((1,), (0,)), ((), ()))


def modp(v):
    q = (v.astype(F32) * INV).astype(I32)
    r = v - q * PRIME
    r = jnp.where(r < 0, r + PRIME, r)
    return jnp.where(r >= PRIME, r - PRIME, r)


def centred(v):
    return jnp.where(v > HALF, v - PRIME, v)


def two_digits(v):
    hi = ((v + 128 + 65536) // 256 - 256) * 256
    return hi, v - hi


def pick_rows(rows, shape):
    at = lax.broadcasted_iota(I32, shape, 0)
    out = jnp.zeros(shape, I32)
    for k, row in enumerate(rows):
        out = jnp.where(at == k, row, out)
    return out.astype(F32)


def index_digits(index, seed):
    x = modp(modp(index * 40503) + seed)
    x = modp(x * x)
    hi, lo = two_digits(centred(modp(x * x)))
    nib = [lax.shift_right_logical(x, jnp.int32(4 * k)) & 15 for k in range(4)]
    one = jnp.ones_like(x)
    return pick_rows(nib + nib + [hi, lo, one, one], (16, index.shape[1]))


def column_digits(index):
    b = modp(index * 29989)
    his, los = [], []
    w = modp(b + b)
    for k in range(4):
        hi, lo = two_digits(centred(w))
        his.append(hi)
        los.append(lo)
        w = modp(w * 16)
    hi, lo = two_digits(centred(modp(modp(b * b) + (12345 - HALF + PRIME))))
    one = jnp.ones_like(b)
    return pick_rows(his + los + [one, one, hi, lo], (16, index.shape[1]))


def residue_digits(v):
    q = (v * INV + MAGIC_ONE) - MAGIC_ONE
    r = v - q * PRIME
    hi = (r + MAGIC_BYTE) - MAGIC_BYTE
    return (r - hi).astype(BF16), hi.astype(BF16)


def joined(parts):
    t = parts[0].astype(I32)
    t = t + lax.shift_left((parts[1] * (1.0 / 256)).astype(I32), jnp.int32(8))
    t = t + lax.shift_left(parts[2].astype(I32), jnp.int32(16))
    return t + lax.shift_left((parts[3] * (1.0 / 256)).astype(I32), jnp.int32(24))


def kernel(
    seeds, ingest, order, out,
    rec, order_in, orders, bdig, xdig, xdig2, gen_a, gen_b, give, sib, mine, red, hint_send, hall, a2,
    tot, tsib, zbuf, full, known,
    s_in, r_in, s_own, s_ord, r_ord, s_sib, r_sib, s_red, r_red, s_hint, r_hint, s_hx, r_hx, s_tot, r_tot,
    s_z, r_z, s_gz, r_gz, s_gx, r_gx, s_gs, r_gs, s_out,
):
    row, col = lax.axis_index("row"), lax.axis_index("col")
    core, x, zl = row % 2, (row // 2) % 4, row // 8
    y, zh = col % 8, col // 8
    z = zh * 4 + zl

    def dev_at(xx, yy, zz, cc):
        return {"row": ((zz % 4) * 4 + xx) * 2 + cc, "col": (zz // 4) * 8 + yy}

    def dev(dx, dy, dz, other):
        return dev_at((x + dx + 4) % 4, (y + dy + 8) % 8, (z + dz + 8) % 8, (core + other) % 2)

    def dev_line(dz):
        return dev_at(x, y, zh * 4 + (zl + dz) % 4, core)

    def rcopy(src, dst, ssem, rsem, device):
        return pltpu.make_async_remote_copy(
            src_ref=src, dst_ref=dst, send_sem=ssem, recv_sem=rsem, device_id=device, device_id_type=MESH
        )

    sibling = dev(0, 0, 0, 1)

    def arrived(spot, rsem):
        rcopy(spot, spot, s_tot, rsem, sibling).wait_recv()

    order_load = pltpu.make_async_copy(order, order_in, s_own)
    order_load.start()

    barrier = pltpu.get_barrier_semaphore()

    def greet(device, sem):
        pl.semaphore_signal(sem, inc=1, device_id=device, device_id_type=MESH)

    count = 1
    greet(sibling, barrier)
    for off in ((0, 1, 0), (0, -1, 0), (1, 0, 0), (-1, 0, 0), (0, 0, 1), (0, 0, -1), (0, 1, 1), (0, -1, -1)):
        for other in range(2):
            greet(dev(*off, other), barrier)
            count += 1
    pl.semaphore_wait(barrier, count)

    def round_send(k):
        dx, dy, dz = ((1, 0, 0), (0, 1, 0), (0, 2, 0), (0, 0, 1), (0, 0, 2))[k]
        greet(dev(dx, dy, dz, 0), known.at[k])
        greet(dev(-dx, -dy, -dz, 0), known.at[k])

    def round_wait(k):
        pl.semaphore_wait(known.at[k], 2)

    colour = (2 * x + y + 3 * z) % 8
    sign = 1 - 2 * core

    def ingest_src(near, other):
        return ingest.at[:, pl.ds(((colour + near) % 8) * 4096 + ((core + other) % 2) * 2048, 2048)]

    def ingest_copy(near, other):
        slot = near * 2 + core
        device = dev(0, sign, sign, other) if near == 4 else dev(*NEAR[near], other)
        return rcopy(
            ingest_src(near, other), rec.at[pl.ds(slot * 16, 16), :],
            s_in.at[near * 2 + other], r_in.at[slot], device,
        )

    for near in ORDER:
        for other in range(2):
            if near or other:
                ingest_copy(near, other).start()
    own_in = pltpu.make_async_copy(ingest_src(0, 0), rec.at[pl.ds(core * 16, 16), :], r_in.at[core])
    own_in.start()
    round_send(0)

    bdig[...] = jnp.transpose(column_digits(lax.broadcasted_iota(I32, (1, 1024), 1))).astype(BF16)
    index = lax.broadcasted_iota(I32, (1, 2048), 1) + (colour * 4096 + core * 2048)
    for w in range(2):
        xdig[w] = index_digits(index, seeds[0] + 7919 * w).astype(BF16)
    round_wait(0)
    round_send(1)

    def generate(buf, t, kh):
        n_at = pl.multiple_of((((1 - core) * 2 + t) % 4) * 256, 256)
        left = bdig[pl.ds(n_at, 256), :]
        for w in range(2):
            digits = xdig[w, :, kh * 1024 : (kh + 1) * 1024]
            lo, hi = residue_digits(lax.dot_general(left, digits, NN, preferred_element_type=F32))
            buf[(2 * w) * 256 : (2 * w + 1) * 256, :] = lo
            buf[(2 * w + 1) * 256 : (2 * w + 2) * 256, :] = hi

    def multiply(buf, kh):
        r = lax.dot_general(buf[...], rec[:, kh * 1024 : (kh + 1) * 1024], NT, preferred_element_type=F32)
        return joined([r[k * 256 : (k + 1) * 256, :] for k in range(4)])

    for kh in range(2):
        generate(gen_a.at[kh], 0, kh)
    round_wait(1)
    round_send(2)

    for slot in range(16):
        arrived(rec.at[pl.ds(slot * 16, 16), :], r_in.at[slot])
    sums = lax.dot_general(jnp.ones((16, 2048), BF16), rec[...], NT, preferred_element_type=F32)
    bias = sums[0:1, :].astype(I32) * jnp.int32(BIAS)

    gens = (gen_a, gen_b)

    def tile(t):
        acc = bias
        for kh in range(2):
            if t < 3:
                generate(gens[(t + 1) % 2].at[kh], t + 1, kh)
            acc = acc + multiply(gens[t % 2].at[kh], kh)
        return jnp.transpose(acc)

    round_wait(2)
    round_send(3)
    give[0] = tile(0)
    round_wait(3)
    round_send(4)
    give[1] = tile(1)
    round_wait(4)
    sib_copy = rcopy(give, sib, s_sib, r_sib, sibling)
    sib_copy.start()

    order_load.wait()
    orders[0, 0] = jnp.broadcast_to(order_in[...], (8, 256))

    def order_copy(k):
        side, dx = k // 4, k % 4
        zz = 7 - z if side else z
        return rcopy(
            orders.at[0, 0], orders.at[side, dx], s_ord.at[k], r_ord.at[k], dev_at((x + dx) % 4, y, zz, core)
        )

    for k in range(1, 8):
        order_copy(k).start()

    def red_copy(q, near):
        if near in (4, 8):
            at, sg = (near // 4 - 1) * 16, 1 if near == 8 else -1
            rows, dst, device = 128 + at, red.at[q, 4, pl.ds(at, 16), :], dev(0, sg, sg, 0)
            rows = mine.at[q, pl.ds(rows, 16), :]
        else:
            dx, dy, dz = NEAR[near]
            rows, dst, device = mine.at[q, pl.ds(near * 32, 32), :], red.at[q, near], dev(-dx, -dy, -dz, 0)
        return rcopy(rows, dst, s_red.at[q * 9 + near], r_red.at[q * 9 + near], device)

    for q in range(2):
        acc = tile(2 + q)
        if q == 0:
            sib_copy.wait_recv()
        mine[q] = acc + sib[q]
        for near in (4, 8, 1, 2, 3, 5, 6, 7):
            red_copy(q, near).start()
    lane = lax.broadcasted_iota(I32, (1, 2048), 1)
    mirrored = (lane // 256) % 2
    block = ((zl + mirrored * (3 - 2 * zl)) * 4 + (x + 4 - lane // 512) % 4) * 2 + core
    for w in range(2):
        xdig2[w] = index_digits(block * 256 + lane % 256, seeds[1] + 7919 * w).astype(BF16)

    for k in range(1, 8):
        arrived(orders.at[k // 4, k % 4], r_ord.at[k])
    spot = lax.broadcasted_iota(I32, (256, 1), 0)
    side = (spot // 64) % 2
    ingest_row = ((zh + side * (1 - 2 * zh)) * 8 + (spot // 8) % 8) * 16 + (spot // 128) * 8 + spot % 8
    wanted = ingest_row + 256 * side
    lane = lax.broadcasted_iota(I32, (1, 512), 1)
    quarter = bdig[pl.ds(pl.multiple_of(x * 256, 256), 256), :]

    def second_rows(dx):
        have = jnp.concatenate([orders[0, dx, 0:1, :], orders[1, dx, 0:1, :]], axis=1) + (lane // 256) * 256
        onehot = (wanted == have).astype(F32).astype(BF16)
        for w in range(2):
            digits = xdig2[w, :, dx * 512 : (dx + 1) * 512]
            perm = lax.dot_general(onehot, digits, NT, preferred_element_type=F32).astype(BF16)
            lo, hi = residue_digits(lax.dot_general(perm, quarter, NT, preferred_element_type=F32))
            a2[2 * w, dx * 256 : (dx + 1) * 256, :] = lo
            a2[2 * w + 1, dx * 256 : (dx + 1) * 256, :] = hi

    second_rows(0)
    second_rows(1)
    hints = []
    for q in range(2):
        hint = mine[q, 0:32, :]
        for near in (1, 2, 3, 5, 6, 7, 4, 8):
            red_copy(q, near).wait_recv()
        for near in range(1, 8):
            hint = hint + red[q, near]
        hints.append(hint)

    low_lane = lax.broadcasted_iota(I32, (8, 128), 1) < 64
    for t in range(4):
        for cc in range(2):
            tile_at = hints[t // 2][cc * 16 : (cc + 1) * 16, (t % 2) * 128 : (t % 2 + 1) * 128]
            top, low = tile_at[0:8, :], tile_at[8:16, :]
            hint_send[2 * t, cc] = jnp.where(low_lane, top, pltpu.roll(low, 64, 1))
            hint_send[2 * t + 1, cc] = jnp.where(low_lane, pltpu.roll(top, 64, 1), low)
    away = (zh + core) % 2
    local = away == 0
    landing = hall.at[0, pl.ds((away * 8 + y) * 8, 8), :]
    landed = r_hint.at[away * 8 + y]

    def hint_copy(dy, other):
        yy = (y + dy) % 8
        return rcopy(
            hint_send.at[yy, (core + other) % 2], landing, s_hint.at[dy * 2 + other], landed,
            dev_at(x, yy, z + away * (7 - 2 * z), (core + other) % 2),
        )

    own_hint = pltpu.make_async_copy(hint_send.at[y, core], landing, landed)
    for dy in (4, 3, 5, 2, 6, 1, 7, 0):
        for other in range(2):
            if dy or other:
                hint_copy(dy, other).start()
            else:
                @pl.when(local)
                def _():
                    own_hint.start()

                @pl.when(jnp.logical_not(local))
                def _():
                    hint_copy(0, 0).start()

    second_rows(3)
    second_rows(2)
    for k in range(16):
        arrived(hall.at[0, pl.ds(k * 8, 8), :], r_hint.at[k])

    def hx_copy(k):
        if k < 2:
            return rcopy(hall.at[0], hall.at[1 + 2 * k], s_hx.at[k], r_hx.at[k], dev(1 - 2 * k, 0, 0, 0))
        at = pl.ds((k - 2) * 64, 64)
        return rcopy(
            hall.at[2 * k - 3, at, :], hall.at[2, at, :], s_hx.at[k], r_hx.at[k], dev(5 - 2 * k, 0, 0, 0)
        )

    for k in range(2):
        hx_copy(k).start()

    def second(dx, total):
        turned = jnp.transpose(hall[dx])
        wide = jnp.concatenate([turned[0:64, :], turned[64:128, :]], axis=1)
        left = jnp.concatenate(
            [
                ((lax.shift_right_logical(wide, jnp.int32(8 * d)) & 255) - 128).astype(F32).astype(BF16)
                for d in range(4)
            ],
            axis=0,
        )
        lsum = lax.dot_general(left, jnp.ones((256, 128), BF16), NN, preferred_element_type=F32)
        term = joined(
            [
                lax.dot_general(left, a2[k, dx * 256 : (dx + 1) * 256, :], NN, preferred_element_type=F32)
                for k in range(4)
            ]
        )
        term = term + lsum[:, 0:1].astype(I32) * jnp.int32(BIAS)
        return term if total is None else total + term

    total = second(0, None)
    hx_copy(0).wait_recv()
    hx_copy(2).start()
    hx_copy(1).wait_recv()
    hx_copy(3).start()
    total = second(1, total)
    total = second(3, total)
    hx_copy(2).wait_recv()
    hx_copy(3).wait_recv()
    total = second(2, total)
    tot[0] = total[:, 0:128]
    tot[1] = total[:, 128:256]

    tot_copy = rcopy(tot.at[1 - core], tsib.at[0], s_tot, r_tot, sibling)
    tot_copy.start()
    tot_copy.wait_recv()
    tsib[1] = tot[core] + tsib[0]

    def z_copy(dz):
        zz = (zl + dz) % 4
        return rcopy(
            tsib.at[1, pl.ds(zz * 64, 64), :], zbuf.at[dz - 1], s_z.at[dz - 1], r_z.at[dz - 1], dev_line(dz)
        )

    for dz in (1, 3, 2):
        z_copy(dz).start()
    acc = tsib[1, pl.ds(pl.multiple_of(zl * 64, 64), 64), :]
    for dz in (1, 3, 2):
        z_copy(dz).wait_recv()
        acc = acc + zbuf[dz - 1]
    full[x, core, pl.ds(pl.multiple_of(zl * 64, 64), 64), :] = acc

    def part_of(dx, j, cc):
        return full.at[(x + 4 - dx) % 4, cc, pl.ds(((zl + 4 - j) % 4) * 64, 64), :]

    def half_of(dx, j, k):
        return full.at[(x + 4 - dx) % 4, core, pl.ds(((zl + 4 - j) % 4) * 64 + k * 32, 32), :]

    def gz_copy(dz):
        return rcopy(part_of(0, 0, core), part_of(0, 0, core), s_gz.at[dz - 1], r_gz.at[dz - 1], dev_line(dz))

    def gx_copy(j, k):
        spot = part_of(0, j, core) if k < 2 else half_of(2 * k - 3, j, k - 2)
        step = 1 - 2 * (k % 2)
        return rcopy(spot, spot, s_gx.at[j * 4 + k], r_gx.at[j * 4 + k], dev(step, 0, 0, 0))

    def out_at(dx, j, cc):
        return out.at[pl.ds(((zl + 4 - j) % 4) * 64, 64), pl.ds(((x + 4 - dx) % 4) * 256 + cc * 128, 128)]

    def gs_copy(dx, j):
        k = dx * 4 + j
        return rcopy(part_of(dx, j, core), out_at(dx, j, core), s_gs.at[k], r_gs.at[k], sibling)

    def out_copy(dx, j):
        return pltpu.make_async_copy(part_of(dx, j, core), out_at(dx, j, core), s_out.at[dx * 4 + j])

    def emit(dx, j):
        gs_copy(dx, j).start()
        out_copy(dx, j).start()

    def spread(j):
        gx_copy(j, 0).start()
        gx_copy(j, 1).start()
        emit(0, j)

    def forward(j):
        arrived(part_of(1, j, core), r_gx.at[j * 4])
        gx_copy(j, 2).start()
        arrived(part_of(3, j, core), r_gx.at[j * 4 + 1])
        gx_copy(j, 3).start()
        emit(1, j)
        emit(3, j)

    def finish(j):
        arrived(half_of(2, j, 0), r_gx.at[j * 4 + 2])
        arrived(half_of(2, j, 1), r_gx.at[j * 4 + 3])
        emit(2, j)

    close = 3 - 2 * (zl // 2)
    chunks = (0, close, 2, 4 - close)
    for dz in (2, 1, 3):
        gz_copy(dz).start()
    spread(0)
    for k in range(1, 4):
        arrived(part_of(0, chunks[k], core), r_gz.at[chunks[k] - 1])
        spread(chunks[k])
        forward(chunks[k - 1])
    forward(chunks[3])
    for j in chunks:
        finish(j)
    for dx in range(4):
        for j in range(4):
            arrived(out_at(dx, j, 1 - core), r_gs.at[dx * 4 + j])

    for near in range(8):
        for other in range(2):
            if near or other:
                ingest_copy(near, other).wait_send()
    for k in range(1, 8):
        order_copy(k).wait_send()
    sib_copy.wait_send()
    for q in range(2):
        for near in range(1, 9):
            red_copy(q, near).wait_send()
    for dy in range(8):
        for other in range(2):
            if dy or other:
                hint_copy(dy, other).wait_send()
            else:
                @pl.when(jnp.logical_not(local))
                def _():
                    hint_copy(0, 0).wait_send()
    for k in range(4):
        hx_copy(k).wait_send()
    tot_copy.wait_send()
    for d in range(1, 4):
        z_copy(d).wait_send()
        gz_copy(d).wait_send()
    for j in range(4):
        for k in range(4):
            gx_copy(j, k).wait_send()
            gs_copy(k, j).wait_send()
    for dx in range(4):
        for j in range(4):
            out_copy(dx, j).wait()


def on_device(ingest, row_order, matrix_seeds):
    dma = pltpu.SemaphoreType.DMA
    scratch = [
        pltpu.VMEM((256, 2048), BF16),
        pltpu.VMEM((1, 256), I32),
        pltpu.VMEM((2, 4, 8, 256), I32),
        pltpu.VMEM((1024, 16), BF16),
        pltpu.VMEM((2, 16, 2048), BF16),
        pltpu.VMEM((2, 16, 2048), BF16),
        pltpu.VMEM((2, 1024, 1024), BF16),
        pltpu.VMEM((2, 1024, 1024), BF16),
        pltpu.VMEM((2, 256, 256), I32),
        pltpu.VMEM((2, 256, 256), I32),
        pltpu.VMEM((2, 256, 256), I32),
        pltpu.VMEM((2, 8, 32, 256), I32),
        pltpu.VMEM((8, 2, 8, 128), I32),
        pltpu.VMEM((4, 128, 128), I32),
        pltpu.VMEM((4, 1024, 256), BF16),
        pltpu.VMEM((2, 256, 128), I32),
        pltpu.VMEM((2, 256, 128), I32),
        pltpu.VMEM((3, 64, 128), I32),
        pltpu.VMEM((4, 2, 256, 128), I32),
        pltpu.SemaphoreType.REGULAR((5,)),
        dma((16,)), dma((16,)), dma, dma((8,)), dma((8,)), dma, dma, dma((18,)), dma((18,)), dma((16,)), dma((16,)),
        dma((4,)), dma((4,)), dma, dma, dma((3,)), dma((3,)), dma((3,)), dma((3,)), dma((16,)), dma((16,)),
        dma((16,)), dma((16,)), dma((16,)),
    ]
    total = pl.pallas_call(
        kernel,
        out_shape=jax.ShapeDtypeStruct((256, 1024), I32),
        in_specs=[
            pl.BlockSpec(memory_space=pltpu.SMEM),
            pl.BlockSpec(memory_space=pltpu.HBM),
            pl.BlockSpec(memory_space=pltpu.HBM),
        ],
        out_specs=pl.BlockSpec(memory_space=pltpu.HBM),
        scratch_shapes=scratch,
        compiler_params=pltpu.CompilerParams(
            collective_id=0, has_side_effects=True, vmem_limit_bytes=60 * 2**20
        ),
        name="hints",
    )(matrix_seeds, ingest, row_order)
    total = total.reshape(4, 64, 1024)
    low = (total & 65535).astype(F32)
    high = lax.shift_right_logical(total, jnp.int32(16)).astype(F32)
    return jnp.stack([low, high], axis=1) * (1.0 / 65536.0)


def solution(mesh):
    return jax.shard_map(
        on_device, mesh=mesh,
        in_specs=(P(("row", "col"), None), P("row", None), P()),
        out_specs=P(None, None, "col", None), check_vma=False,
    )
```

```python
import functools

import jax
import jax.numpy as jnp
from jax import lax
from jax.experimental import pallas as pl
from jax.experimental.pallas import tpu as pltpu
from jax.sharding import PartitionSpec as P

PRIME = 46337
HALF = 23168
INV = 1.0 / PRIME
MAGIC_ONE = 1.5 * 2.0**23
MAGIC_BYTE = 1.5 * 2.0**31
BIAS = (HALF * 65537 - 0x80808080) % 2**32
BIAS = BIAS - 2**32 if BIAS >= 2**31 else BIAS
NEAR = ((0, 0, 0), (0, 1, 0), (1, 0, 0), (0, 0, 1), (0, 1, 1), (0, 0, -1), (-1, 0, 0), (0, -1, 0))
ORDER = (4, 1, 2, 3, 5, 6, 7, 0)
MESH = pl.DeviceIdType.MESH
F32, BF16, I32 = jnp.float32, jnp.bfloat16, jnp.int32
NT = (((1,), (1,)), ((), ()))
NN = (((1,), (0,)), ((), ()))


def modp(v):
    q = (v.astype(F32) * INV).astype(I32)
    r = v - q * PRIME
    r = jnp.where(r < 0, r + PRIME, r)
    return jnp.where(r >= PRIME, r - PRIME, r)


def centred(v):
    return jnp.where(v > HALF, v - PRIME, v)


def two_digits(v):
    hi = ((v + 128 + 65536) // 256 - 256) * 256
    return hi, v - hi


def pick_rows(rows, shape):
    at = lax.broadcasted_iota(I32, shape, 0)
    out = jnp.zeros(shape, I32)
    for k, row in enumerate(rows):
        out = jnp.where(at == k, row, out)
    return out.astype(F32)


def index_digits(index, seed):
    x = modp(modp(index * 40503) + seed)
    x = modp(x * x)
    hi, lo = two_digits(centred(modp(x * x)))
    nib = [lax.shift_right_logical(x, jnp.int32(4 * k)) & 15 for k in range(4)]
    one = jnp.ones_like(x)
    return pick_rows(nib + nib + [hi, lo, one, one], (16, index.shape[1]))


def column_digits(index):
    b = modp(index * 29989)
    his, los = [], []
    w = modp(b + b)
    for k in range(4):
        hi, lo = two_digits(centred(w))
        his.append(hi)
        los.append(lo)
        w = modp(w * 16)
    hi, lo = two_digits(centred(modp(modp(b * b) + (12345 - HALF + PRIME))))
    one = jnp.ones_like(b)
    return pick_rows(his + los + [one, one, hi, lo], (16, index.shape[1]))


def residue_digits(v):
    q = (v * INV + MAGIC_ONE) - MAGIC_ONE
    r = v - q * PRIME
    hi = (r + MAGIC_BYTE) - MAGIC_BYTE
    return (r - hi).astype(BF16), hi.astype(BF16)


def joined(parts):
    t = parts[0].astype(I32)
    t = t + lax.shift_left((parts[1] * (1.0 / 256)).astype(I32), jnp.int32(8))
    t = t + lax.shift_left(parts[2].astype(I32), jnp.int32(16))
    return t + lax.shift_left((parts[3] * (1.0 / 256)).astype(I32), jnp.int32(24))


def kernel(
    seeds, ingest, order, out,
    rec, order_in, orders, bdig, xdig, xdig2, gen_a, gen_b, give, sib, mine, red, hint_send, hall, a2,
    tot, tsib, zbuf, full, known,
    s_in, r_in, s_own, s_ord, r_ord, s_sib, r_sib, s_red, r_red, s_hint, r_hint, s_hx, r_hx, s_tot, r_tot,
    s_z, r_z, s_gz, r_gz, s_gx, r_gx, s_gs, r_gs, s_out,
):
    row, col = lax.axis_index("row"), lax.axis_index("col")
    core, x, zl = row % 2, (row // 2) % 4, row // 8
    y, zh = col % 8, col // 8
    z = zh * 4 + zl

    def dev_at(xx, yy, zz, cc):
        return {"row": ((zz % 4) * 4 + xx) * 2 + cc, "col": (zz // 4) * 8 + yy}

    def dev(dx, dy, dz, other):
        return dev_at((x + dx + 4) % 4, (y + dy + 8) % 8, (z + dz + 8) % 8, (core + other) % 2)

    def dev_line(dz):
        return dev_at(x, y, zh * 4 + (zl + dz) % 4, core)

    def rcopy(src, dst, ssem, rsem, device):
        return pltpu.make_async_remote_copy(
            src_ref=src, dst_ref=dst, send_sem=ssem, recv_sem=rsem, device_id=device, device_id_type=MESH
        )

    sibling = dev(0, 0, 0, 1)

    def arrived(spot, rsem):
        rcopy(spot, spot, s_tot, rsem, sibling).wait_recv()

    order_load = pltpu.make_async_copy(order, order_in, s_own)
    order_load.start()

    barrier = pltpu.get_barrier_semaphore()

    def greet(device, sem):
        pl.semaphore_signal(sem, inc=1, device_id=device, device_id_type=MESH)

    count = 1
    greet(sibling, barrier)
    for off in ((0, 1, 0), (0, -1, 0), (1, 0, 0), (-1, 0, 0), (0, 0, 1), (0, 0, -1), (0, 1, 1), (0, -1, -1)):
        for other in range(2):
            greet(dev(*off, other), barrier)
            count += 1
    pl.semaphore_wait(barrier, count)

    def round_send(k):
        dx, dy, dz = ((1, 0, 0), (0, 1, 0), (0, 2, 0), (0, 0, 1), (0, 0, 2))[k]
        greet(dev(dx, dy, dz, 0), known.at[k])
        greet(dev(-dx, -dy, -dz, 0), known.at[k])

    def round_wait(k):
        pl.semaphore_wait(known.at[k], 2)

    colour = (2 * x + y + 3 * z) % 8
    sign = 1 - 2 * core

    def ingest_src(near, other):
        return ingest.at[:, pl.ds(((colour + near) % 8) * 4096 + ((core + other) % 2) * 2048, 2048)]

    def ingest_copy(near, other):
        slot = near * 2 + core
        device = dev(0, sign, sign, other) if near == 4 else dev(*NEAR[near], other)
        return rcopy(
            ingest_src(near, other), rec.at[pl.ds(slot * 16, 16), :],
            s_in.at[near * 2 + other], r_in.at[slot], device,
        )

    for near in ORDER:
        for other in range(2):
            if near or other:
                ingest_copy(near, other).start()
    own_in = pltpu.make_async_copy(ingest_src(0, 0), rec.at[pl.ds(core * 16, 16), :], r_in.at[core])
    own_in.start()
    round_send(0)

    bdig[...] = jnp.transpose(column_digits(lax.broadcasted_iota(I32, (1, 1024), 1))).astype(BF16)
    index = lax.broadcasted_iota(I32, (1, 2048), 1) + (colour * 4096 + core * 2048)
    for w in range(2):
        xdig[w] = index_digits(index, seeds[0] + 7919 * w).astype(BF16)
    round_wait(0)
    round_send(1)

    def generate(buf, t, kh):
        n_at = pl.multiple_of((((1 - core) * 2 + t) % 4) * 256, 256)
        left = bdig[pl.ds(n_at, 256), :]
        for w in range(2):
            digits = xdig[w, :, kh * 1024 : (kh + 1) * 1024]
            lo, hi = residue_digits(lax.dot_general(left, digits, NN, preferred_element_type=F32))
            buf[(2 * w) * 256 : (2 * w + 1) * 256, :] = lo
            buf[(2 * w + 1) * 256 : (2 * w + 2) * 256, :] = hi

    def multiply(buf, kh):
        r = lax.dot_general(buf[...], rec[:, kh * 1024 : (kh + 1) * 1024], NT, preferred_element_type=F32)
        return joined([r[k * 256 : (k + 1) * 256, :] for k in range(4)])

    for kh in range(2):
        generate(gen_a.at[kh], 0, kh)
    generate(gen_b.at[0], 1, 0)
    round_wait(1)
    round_send(2)

    for slot in range(16):
        arrived(rec.at[pl.ds(slot * 16, 16), :], r_in.at[slot])
    sums = lax.dot_general(jnp.ones((16, 2048), BF16), rec[...], NT, preferred_element_type=F32)
    bias = sums[0:1, :].astype(I32) * jnp.int32(BIAS)

    gens = (gen_a, gen_b)

    def tile(t):
        acc = bias
        for kh in range(2):
            if t < 3 and (t or kh):
                generate(gens[(t + 1) % 2].at[kh], t + 1, kh)
            acc = acc + multiply(gens[t % 2].at[kh], kh)
        return jnp.transpose(acc)

    round_wait(2)
    round_send(3)
    give[0] = tile(0)
    round_wait(3)
    round_send(4)
    give[1] = tile(1)
    round_wait(4)
    sib_copy = rcopy(give, sib, s_sib, r_sib, sibling)
    sib_copy.start()

    order_load.wait()
    orders[0, 0] = jnp.broadcast_to(order_in[...], (8, 256))

    def order_copy(k):
        side, dx = k // 4, k % 4
        zz = 7 - z if side else z
        return rcopy(
            orders.at[0, 0], orders.at[side, dx], s_ord.at[k], r_ord.at[k], dev_at((x + dx) % 4, y, zz, core)
        )

    for k in range(1, 8):
        order_copy(k).start()

    def red_copy(q, near):
        if near in (4, 8):
            at, sg = (near // 4 - 1) * 16, 1 if near == 8 else -1
            rows, dst, device = 128 + at, red.at[q, 4, pl.ds(at, 16), :], dev(0, sg, sg, 0)
            rows = mine.at[q, pl.ds(rows, 16), :]
        else:
            dx, dy, dz = NEAR[near]
            rows, dst, device = mine.at[q, pl.ds(near * 32, 32), :], red.at[q, near], dev(-dx, -dy, -dz, 0)
        return rcopy(rows, dst, s_red.at[q * 9 + near], r_red.at[q * 9 + near], device)

    for q in range(2):
        acc = tile(2 + q)
        if q == 0:
            sib_copy.wait_recv()
        mine[q] = acc + sib[q]
        for near in (4, 8, 1, 2, 3, 5, 6, 7):
            red_copy(q, near).start()
    lane = lax.broadcasted_iota(I32, (1, 2048), 1)
    mirrored = (lane // 256) % 2
    block = ((zl + mirrored * (3 - 2 * zl)) * 4 + (x + 4 - lane // 512) % 4) * 2 + core
    for w in range(2):
        xdig2[w] = index_digits(block * 256 + lane % 256, seeds[1] + 7919 * w).astype(BF16)

    for k in range(1, 8):
        arrived(orders.at[k // 4, k % 4], r_ord.at[k])
    spot = lax.broadcasted_iota(I32, (256, 1), 0)
    side = (spot // 64) % 2
    ingest_row = ((zh + side * (1 - 2 * zh)) * 8 + (spot // 8) % 8) * 16 + (spot // 128) * 8 + spot % 8
    wanted = ingest_row + 256 * side
    lane = lax.broadcasted_iota(I32, (1, 512), 1)
    quarter = bdig[pl.ds(pl.multiple_of(x * 256, 256), 256), :]

    def second_rows(dx):
        have = jnp.concatenate([orders[0, dx, 0:1, :], orders[1, dx, 0:1, :]], axis=1) + (lane // 256) * 256
        onehot = (wanted == have).astype(F32).astype(BF16)
        for w in range(2):
            digits = xdig2[w, :, dx * 512 : (dx + 1) * 512]
            perm = lax.dot_general(onehot, digits, NT, preferred_element_type=F32).astype(BF16)
            lo, hi = residue_digits(lax.dot_general(perm, quarter, NT, preferred_element_type=F32))
            a2[2 * w, dx * 256 : (dx + 1) * 256, :] = lo
            a2[2 * w + 1, dx * 256 : (dx + 1) * 256, :] = hi

    second_rows(0)
    second_rows(1)
    hints = []
    for q in range(2):
        hint = mine[q, 0:32, :]
        for near in (1, 2, 3, 5, 6, 7, 4, 8):
            red_copy(q, near).wait_recv()
        for near in range(1, 8):
            hint = hint + red[q, near]
        hints.append(hint)

    low_lane = lax.broadcasted_iota(I32, (8, 128), 1) < 64
    for t in range(4):
        for cc in range(2):
            tile_at = hints[t // 2][cc * 16 : (cc + 1) * 16, (t % 2) * 128 : (t % 2 + 1) * 128]
            top, low = tile_at[0:8, :], tile_at[8:16, :]
            hint_send[2 * t, cc] = jnp.where(low_lane, top, pltpu.roll(low, 64, 1))
            hint_send[2 * t + 1, cc] = jnp.where(low_lane, pltpu.roll(top, 64, 1), low)
    away = (zh + core) % 2
    local = away == 0
    landing = hall.at[0, pl.ds((away * 8 + y) * 8, 8), :]
    landed = r_hint.at[away * 8 + y]

    def hint_copy(dy, other):
        yy = (y + dy) % 8
        return rcopy(
            hint_send.at[yy, (core + other) % 2], landing, s_hint.at[dy * 2 + other], landed,
            dev_at(x, yy, z + away * (7 - 2 * z), (core + other) % 2),
        )

    own_hint = pltpu.make_async_copy(hint_send.at[y, core], landing, landed)
    for dy in (4, 3, 5, 2, 6, 1, 7, 0):
        for other in range(2):
            if dy or other:
                hint_copy(dy, other).start()
            else:
                @pl.when(local)
                def _():
                    own_hint.start()

                @pl.when(jnp.logical_not(local))
                def _():
                    hint_copy(0, 0).start()

    second_rows(3)
    second_rows(2)
    for k in range(16):
        arrived(hall.at[0, pl.ds(k * 8, 8), :], r_hint.at[k])

    def hx_copy(k):
        if k < 2:
            return rcopy(hall.at[0], hall.at[1 + 2 * k], s_hx.at[k], r_hx.at[k], dev(1 - 2 * k, 0, 0, 0))
        at = pl.ds((k - 2) * 64, 64)
        return rcopy(
            hall.at[2 * k - 3, at, :], hall.at[2, at, :], s_hx.at[k], r_hx.at[k], dev(5 - 2 * k, 0, 0, 0)
        )

    for k in range(2):
        hx_copy(k).start()

    def second(dx, total):
        turned = jnp.transpose(hall[dx])
        wide = jnp.concatenate([turned[0:64, :], turned[64:128, :]], axis=1)
        left = jnp.concatenate(
            [
                ((lax.shift_right_logical(wide, jnp.int32(8 * d)) & 255) - 128).astype(F32).astype(BF16)
                for d in range(4)
            ],
            axis=0,
        )
        lsum = lax.dot_general(left, jnp.ones((256, 128), BF16), NN, preferred_element_type=F32)
        term = joined(
            [
                lax.dot_general(left, a2[k, dx * 256 : (dx + 1) * 256, :], NN, preferred_element_type=F32)
                for k in range(4)
            ]
        )
        term = term + lsum[:, 0:1].astype(I32) * jnp.int32(BIAS)
        return term if total is None else total + term

    total = second(0, None)
    hx_copy(0).wait_recv()
    hx_copy(2).start()
    hx_copy(1).wait_recv()
    hx_copy(3).start()
    total = second(1, total)
    total = second(3, total)
    hx_copy(2).wait_recv()
    hx_copy(3).wait_recv()
    total = second(2, total)
    tot[0] = total[:, 0:128]
    tot[1] = total[:, 128:256]

    tot_copy = rcopy(tot.at[1 - core], tsib.at[0], s_tot, r_tot, sibling)
    tot_copy.start()
    tot_copy.wait_recv()
    tsib[1] = tot[core] + tsib[0]

    def z_copy(dz):
        zz = (zl + dz) % 4
        return rcopy(
            tsib.at[1, pl.ds(zz * 64, 64), :], zbuf.at[dz - 1], s_z.at[dz - 1], r_z.at[dz - 1], dev_line(dz)
        )

    for dz in (1, 3, 2):
        z_copy(dz).start()
    acc = tsib[1, pl.ds(pl.multiple_of(zl * 64, 64), 64), :]
    for dz in (1, 3, 2):
        z_copy(dz).wait_recv()
        acc = acc + zbuf[dz - 1]
    full[x, core, pl.ds(pl.multiple_of(zl * 64, 64), 64), :] = acc

    def part_of(dx, j, cc):
        return full.at[(x + 4 - dx) % 4, cc, pl.ds(((zl + 4 - j) % 4) * 64, 64), :]

    def half_of(dx, j, k):
        return full.at[(x + 4 - dx) % 4, core, pl.ds(((zl + 4 - j) % 4) * 64 + k * 32, 32), :]

    def gz_copy(dz):
        return rcopy(part_of(0, 0, core), part_of(0, 0, core), s_gz.at[dz - 1], r_gz.at[dz - 1], dev_line(dz))

    def gx_copy(j, k):
        spot = part_of(0, j, core) if k < 2 else half_of(2 * k - 3, j, k - 2)
        step = 1 - 2 * (k % 2)
        return rcopy(spot, spot, s_gx.at[j * 4 + k], r_gx.at[j * 4 + k], dev(step, 0, 0, 0))

    def out_at(dx, j, cc):
        return out.at[pl.ds(((zl + 4 - j) % 4) * 64, 64), pl.ds(((x + 4 - dx) % 4) * 256 + cc * 128, 128)]

    def gs_copy(dx, j):
        k = dx * 4 + j
        return rcopy(part_of(dx, j, core), out_at(dx, j, core), s_gs.at[k], r_gs.at[k], sibling)

    def out_copy(dx, j):
        return pltpu.make_async_copy(part_of(dx, j, core), out_at(dx, j, core), s_out.at[dx * 4 + j])

    def emit(dx, j):
        gs_copy(dx, j).start()
        out_copy(dx, j).start()

    def spread(j):
        gx_copy(j, 0).start()
        gx_copy(j, 1).start()
        emit(0, j)

    def forward(j):
        arrived(part_of(1, j, core), r_gx.at[j * 4])
        gx_copy(j, 2).start()
        arrived(part_of(3, j, core), r_gx.at[j * 4 + 1])
        gx_copy(j, 3).start()
        emit(1, j)
        emit(3, j)

    def finish(j):
        arrived(half_of(2, j, 0), r_gx.at[j * 4 + 2])
        arrived(half_of(2, j, 1), r_gx.at[j * 4 + 3])
        emit(2, j)

    close = 3 - 2 * (zl // 2)
    chunks = (0, close, 2, 4 - close)
    for dz in (2, 1, 3):
        gz_copy(dz).start()
    spread(0)
    for k in range(1, 4):
        arrived(part_of(0, chunks[k], core), r_gz.at[chunks[k] - 1])
        spread(chunks[k])
        forward(chunks[k - 1])
    forward(chunks[3])
    for j in chunks:
        finish(j)
    for dx in range(4):
        for j in range(4):
            arrived(out_at(dx, j, 1 - core), r_gs.at[dx * 4 + j])

    for near in range(8):
        for other in range(2):
            if near or other:
                ingest_copy(near, other).wait_send()
    for k in range(1, 8):
        order_copy(k).wait_send()
    sib_copy.wait_send()
    for q in range(2):
        for near in range(1, 9):
            red_copy(q, near).wait_send()
    for dy in range(8):
        for other in range(2):
            if dy or other:
                hint_copy(dy, other).wait_send()
            else:
                @pl.when(jnp.logical_not(local))
                def _():
                    hint_copy(0, 0).wait_send()
    for k in range(4):
        hx_copy(k).wait_send()
    tot_copy.wait_send()
    for d in range(1, 4):
        z_copy(d).wait_send()
        gz_copy(d).wait_send()
    for j in range(4):
        for k in range(4):
            gx_copy(j, k).wait_send()
            gs_copy(k, j).wait_send()
    for dx in range(4):
        for j in range(4):
            out_copy(dx, j).wait()


def on_device(ingest, row_order, matrix_seeds):
    dma = pltpu.SemaphoreType.DMA
    scratch = [
        pltpu.VMEM((256, 2048), BF16),
        pltpu.VMEM((1, 256), I32),
        pltpu.VMEM((2, 4, 8, 256), I32),
        pltpu.VMEM((1024, 16), BF16),
        pltpu.VMEM((2, 16, 2048), BF16),
        pltpu.VMEM((2, 16, 2048), BF16),
        pltpu.VMEM((2, 1024, 1024), BF16),
        pltpu.VMEM((2, 1024, 1024), BF16),
        pltpu.VMEM((2, 256, 256), I32),
        pltpu.VMEM((2, 256, 256), I32),
        pltpu.VMEM((2, 256, 256), I32),
        pltpu.VMEM((2, 8, 32, 256), I32),
        pltpu.VMEM((8, 2, 8, 128), I32),
        pltpu.VMEM((4, 128, 128), I32),
        pltpu.VMEM((4, 1024, 256), BF16),
        pltpu.VMEM((2, 256, 128), I32),
        pltpu.VMEM((2, 256, 128), I32),
        pltpu.VMEM((3, 64, 128), I32),
        pltpu.VMEM((4, 2, 256, 128), I32),
        pltpu.SemaphoreType.REGULAR((5,)),
        dma((16,)), dma((16,)), dma, dma((8,)), dma((8,)), dma, dma, dma((18,)), dma((18,)), dma((16,)), dma((16,)),
        dma((4,)), dma((4,)), dma, dma, dma((3,)), dma((3,)), dma((3,)), dma((3,)), dma((16,)), dma((16,)),
        dma((16,)), dma((16,)), dma((16,)),
    ]
    total = pl.pallas_call(
        kernel,
        out_shape=jax.ShapeDtypeStruct((256, 1024), I32),
        in_specs=[
            pl.BlockSpec(memory_space=pltpu.SMEM),
            pl.BlockSpec(memory_space=pltpu.HBM),
            pl.BlockSpec(memory_space=pltpu.HBM),
        ],
        out_specs=pl.BlockSpec(memory_space=pltpu.HBM),
        scratch_shapes=scratch,
        compiler_params=pltpu.CompilerParams(
            collective_id=0, has_side_effects=True, vmem_limit_bytes=60 * 2**20
        ),
        name="hints",
    )(matrix_seeds, ingest, row_order)
    total = total.reshape(4, 64, 1024)
    low = (total & 65535).astype(F32)
    high = lax.shift_right_logical(total, jnp.int32(16)).astype(F32)
    return jnp.stack([low, high], axis=1) * (1.0 / 65536.0)


def solution(mesh):
    return jax.shard_map(
        on_device, mesh=mesh,
        in_specs=(P(("row", "col"), None), P("row", None), P()),
        out_specs=P(None, None, "col", None), check_vma=False,
    )
```
